256 devices in a mesh: seq: 128 (over y, z, x), head: 2 (over core).
Axes of the slice: x: 4, y: 4, z: 8, core: 2. Of those that a mesh axis runs over, the one named last changes fastest.
Arguments:
- query_input: bfloat16 [65536, 1536], P('seq', 'head'), may hold values from -400 to 400
- key_input: bfloat16 [65536, 1536], P('seq', 'head'), may hold values from -40 to 40
- value_input: bfloat16 [65536, 1536], P('seq', 'head'), may hold values from -60 to 60
- cube_lists: int32 [1024, 12, 32], P('seq', 'head'), may hold values from 0 to 1023, as said below
- coarse_gate: float32 [12], P('head'), may hold values from 0.5 to 2
- out_weight: bfloat16 [1536, 1536], replicated, may hold values from -0.875 to 0.875
Outputs:
- mixed_out: bfloat16 [65536, 1536], P('seq', 'head')
The draws below stay inside these ranges and needn't reach their ends.
Inputs may be any that keep to these rules, and one draw needn't show every extreme that they name: `cube_lists`: A list holds 32 distinct cubes and never a cube of the query's own block of 8 cubes (the cubes of one index of seq). For each such block and each half of the heads, the distinct (head, key cube) pairs that the block's lists name among the cubes of one other block number at most 3; 3 is reached in every draw. Lists favour some blocks over others.
All inputs are finite; a program needn't handle non-finite values.
Results may differ from the reference program's by a relative error of at most 0.0054.
Values may be sent and summed in bfloat16 or wider, within the bound.
A program may use at most 128 MiB of HBM per device.

```python
import jax
import jax.numpy as jnp
from jax import lax

D = 1536
HEADS = 12
HD = 128
CUBE = 64
TOPK = 32
CUBE_DEV = 8
HEADS_DEV = 6
CUBES = 1024
TOKENS = 65536
CAP = 3


def common_parts(key):
    key_common = jax.random.normal(jax.random.fold_in(key, 201), (CUBES, 1, HEADS, HD), jnp.float32)
    key_jitter = jax.random.normal(jax.random.fold_in(key, 202), (CUBES, CUBE, HEADS, HD), jnp.float32)
    return (key_common, key_jitter)


def draw_key_input(key, part):
    base_key = key
    key_common, key_jitter = common_parts(base_key)
    rough = 1.5 * key_common + 1.5 * key_jitter
    return rough.reshape(TOKENS, D).astype(jnp.bfloat16)


def draw_query_input(key, part):
    key = jax.random.fold_in(key, 5)
    query_common = jax.random.normal(jax.random.fold_in(key, 1), (CUBES, 1, HEADS, HD), jnp.float32)
    query_jitter = jax.random.normal(jax.random.fold_in(key, 2), (CUBES, CUBE, HEADS, HD), jnp.float32)
    rough = 1.5 * query_common + 0.5 * query_jitter
    return rough.reshape(TOKENS, D).astype(jnp.bfloat16)


def draw_value_input(key, part):
    key = jax.random.fold_in(key, 9)
    value_common = jax.random.normal(jax.random.fold_in(key, 1), (CUBES, 1, HEADS, HD), jnp.float32)
    value_jitter = jax.random.normal(jax.random.fold_in(key, 2), (CUBES, CUBE, HEADS, HD), jnp.float32)
    result = value_common + value_jitter
    return result.reshape(TOKENS, D).astype(jnp.bfloat16)


def draw_cube_lists(key, part):
    key = jax.random.fold_in(key, 7)
    block_count = CUBES // CUBE_DEV
    group_count = HEADS // HEADS_DEV
    slot_count = block_count * CAP
    cand_count = slot_count // HEADS_DEV
    order_scores = jax.random.randint(jax.random.fold_in(key, 1), (block_count, group_count, HEADS_DEV), 0, 1 << 20)
    order_scores = order_scores * HEADS_DEV + jnp.arange(HEADS_DEV, dtype=jnp.int32)
    head_order = jnp.argsort(order_scores, axis=-1).astype(jnp.int32)
    inverse = jnp.argsort(head_order, axis=-1).astype(jnp.int32)
    cube_shift = jax.random.randint(jax.random.fold_in(key, 2), (block_count, group_count, block_count), 0, CUBE_DEV)
    cand_iota = jnp.arange(cand_count, dtype=jnp.int32)
    slot_index = cand_iota[None, None, None, :] * HEADS_DEV + inverse[:, :, :, None]
    owners = slot_index // CAP
    owner_shift = jnp.take_along_axis(cube_shift, owners.reshape(block_count, group_count, -1), axis=2)
    owner_shift = owner_shift.reshape(owners.shape)
    within = (slot_index // HEADS_DEV + owner_shift) % CUBE_DEV
    candidates = owners * CUBE_DEV + within
    block_iota = jnp.arange(block_count, dtype=jnp.int32)
    hot_owner = (block_iota + 1 + jax.random.randint(jax.random.fold_in(key, 3), (block_count,), 0, block_count - 1)) % block_count
    heat_level = jax.random.randint(jax.random.fold_in(key, 4), (block_count,), 0, 3)
    levels = heat_level[owners]
    levels = jnp.where(owners == hot_owner[:, None, None, None], 3, levels)
    levels = jnp.where(owners == block_iota[:, None, None, None], -1, levels)
    jitter = jax.random.randint(jax.random.fold_in(key, 5), (block_count, CUBE_DEV, group_count, HEADS_DEV, cand_count), 0, 1 << 19)
    scores = (levels[:, None] + 1) * (1 << 19) + jitter
    keyed = scores * cand_count + cand_iota
    picked = lax.top_k(keyed, TOPK)[1].astype(jnp.int32)
    spread = jnp.broadcast_to(candidates[:, None], (block_count, CUBE_DEV, group_count, HEADS_DEV, cand_count))
    chosen = jnp.take_along_axis(spread, picked, axis=-1)
    return chosen.reshape(CUBES, HEADS, TOPK).astype(jnp.int32)


def steps_of(stream_key, shape, shards, smallest, top_value):
    factor_of = 1.0
    for position, parts in shards:
        heights = jax.random.uniform(jax.random.fold_in(jax.random.fold_in(stream_key, 6), position), (parts,), jnp.float32, smallest / len(shards), top_value / len(shards))
        factor_of = factor_of * jnp.repeat(jnp.exp(heights), shape[position] // parts).reshape((-1,) + (1,) * (len(shape) - 1 - position))
    return factor_of


def noise(own_key, shape, deviation, reach, kind=jnp.bfloat16):
    values = deviation * jax.random.normal(own_key, shape, jnp.float32)
    return jnp.clip(values, min=-reach, max=reach).astype(kind)


def setup_inputs(seed: int = 0) -> dict:
    streams_of = jax.random.split(jax.random.key(seed), 7)
    query_input = draw_query_input(jax.random.fold_in(streams_of[6], 71), 0)
    key_input = draw_key_input(jax.random.fold_in(streams_of[6], 71), 0)
    value_input = draw_value_input(jax.random.fold_in(streams_of[6], 71), 0)
    cube_lists = draw_cube_lists(jax.random.fold_in(streams_of[6], 71), 0)
    coarse_gate = jnp.clip(0.5 + 1.5 * jax.random.uniform(streams_of[4], (HEADS,), jnp.float32) ** steps_of(streams_of[4], (HEADS,), ((0, 2),), -0.2, 0.2), 0.5, 2.0)
    out_weight = noise(streams_of[5], (D, D), (D // 32) ** -0.5, 0.875)
    return {"query_input": query_input, "key_input": key_input, "value_input": value_input, "cube_lists": cube_lists, "coarse_gate": coarse_gate, "out_weight": out_weight}


def reference(query_input, key_input, value_input, cube_lists, coarse_gate, out_weight):
    score_scale = HD ** -0.5
    block_cubes = 4
    query_cubes = query_input.reshape(CUBES, CUBE, HEADS, HD)
    key_cubes = key_input.reshape(CUBES, CUBE, HEADS, HD)
    value_cubes = value_input.reshape(CUBES, CUBE, HEADS, HD)
    pooled_q = jnp.mean(query_cubes.astype(jnp.float32), axis=1)
    pooled_k = jnp.mean(key_cubes.astype(jnp.float32), axis=1)
    pooled_v = jnp.mean(value_cubes.astype(jnp.float32), axis=1)
    coarse_scores = jnp.einsum("chd,nhd->chn", pooled_q, pooled_k, precision=lax.Precision.HIGHEST) * score_scale
    coarse_weights = lax.optimization_barrier(jax.nn.softmax(coarse_scores, axis=-1).astype(jnp.bfloat16))
    coarse = jnp.einsum("chn,nhd->chd", coarse_weights.astype(jnp.float32), pooled_v, precision=lax.Precision.HIGHEST)
    keys_by_head = jnp.transpose(key_cubes, (0, 2, 1, 3))
    values_by_head = jnp.transpose(value_cubes, (0, 2, 1, 3))
    head_iota = jnp.arange(HEADS, dtype=jnp.int32)[None, :, None]

    def fine_block(block_index):
        row_start = (block_index * block_cubes).astype(jnp.int32)
        block_q = lax.dynamic_slice_in_dim(query_cubes, row_start, block_cubes, 0).astype(jnp.float32)
        block_lists = lax.dynamic_slice_in_dim(cube_lists, row_start, block_cubes, 0)
        remote_k = keys_by_head[block_lists, head_iota].astype(jnp.float32)
        remote_v = values_by_head[block_lists, head_iota].astype(jnp.float32)
        own_k = lax.dynamic_slice_in_dim(keys_by_head, row_start, block_cubes, 0).astype(jnp.float32)
        own_v = lax.dynamic_slice_in_dim(values_by_head, row_start, block_cubes, 0).astype(jnp.float32)
        remote_scores = jnp.einsum("gqhd,ghtkd->ghqtk", block_q, remote_k) * score_scale
        remote_scores = remote_scores.reshape(block_cubes, HEADS, CUBE, TOPK * CUBE)
        own_scores = jnp.einsum("gqhd,ghkd->ghqk", block_q, own_k) * score_scale
        joined = jnp.concatenate([remote_scores, own_scores], axis=-1)
        weights = lax.optimization_barrier(jax.nn.softmax(joined, axis=-1).astype(jnp.bfloat16)).astype(jnp.float32)
        remote_w = weights[..., :TOPK * CUBE].reshape(block_cubes, HEADS, CUBE, TOPK, CUBE)
        own_w = weights[..., TOPK * CUBE:]
        return jnp.einsum("ghqtk,ghtkd->gqhd", remote_w, remote_v) + jnp.einsum("ghqk,ghkd->gqhd", own_w, own_v)

    fine_out = lax.map(fine_block, jnp.arange(CUBES // block_cubes, dtype=jnp.int32))
    fine_out = fine_out.reshape(CUBES, CUBE, HEADS, HD)
    attended = fine_out + coarse_gate[None, None, :, None] * coarse[:, None, :, :]
    attended = attended.astype(jnp.bfloat16).reshape(TOKENS, D)
    return jnp.dot(attended, out_weight, preferred_element_type=jnp.float32).astype(jnp.bfloat16)
```

```python
import functools

import jax
import jax.numpy as jnp
from jax import lax
from jax.experimental import pallas as pl
from jax.experimental.pallas import tpu as pltpu
from jax.sharding import PartitionSpec as P

NX, NY, NZ = 4, 4, 8
PLANE = NX * NY
SLOTS = 3
CUBES = 8
HEADS = 6
TOK = 64
HD = 128
TOP = 32
UNITS = CUBES * HEADS
MAXU = 224
GROUP = 16
RING = MAXU // GROUP + 1
NEG = -1e30
AHEAD = 4
PACK = SLOTS * TOK
SCALE = HD ** -0.5
LOG2E = 1.4426950408889634
NT = (((1,), (1,)), ((), ()))


def iota(shape, dim):
    return lax.broadcasted_iota(jnp.int32, shape, dim)


def flag(mask):
    return jnp.where(mask, 1.0, 0.0).astype(jnp.bfloat16)


def unit_slots(lists_ref, table_ref, bits_ref, rank_ref):
    entry_bit = 1 << (iota((CUBES, 256), 1) >> 5)
    bits = []
    for h in range(HEADS):
        row = lists_ref[h:h + 1, :]
        owner_hot = flag((row >> 3) == iota((128, 256), 0))
        within_bit = jnp.where((row & 7) == iota((CUBES, 256), 0), entry_bit, 0)
        bits.append(lax.dot_general(within_bit.astype(jnp.float32).astype(jnp.bfloat16), owner_hot, NT,
                                    preferred_element_type=jnp.float32))
    bits = jnp.concatenate(bits, axis=0)
    need = bits > 0
    lower = flag(iota((UNITS, UNITS), 0) >= iota((UNITS, UNITS), 1))
    rank = jnp.dot(lower, flag(need), preferred_element_type=jnp.float32)
    bits_ref[...] = bits
    rank_ref[...] = rank
    unit = iota((UNITS, 128), 0)
    table_ref[...] = jnp.zeros_like(table_ref)
    for s in range(SLOTS):
        table_ref[s:s + 1, :] = jnp.sum(jnp.where(need & (rank == s + 1), unit, 0), axis=0, keepdims=True)


def head_lists(bits_ref, rank_ref, count_ref, slots_ref, cubes_ref):
    bits, rank = bits_ref[...], rank_ref[...]
    need = bits > 0
    mine, mine_bits = [], []
    for s in range(SLOTS):
        hit = jnp.where(need & (rank == s + 1), 1.0, 0.0)
        seen = hit * bits
        mine.append([jnp.sum(hit[h * 8:h * 8 + 8], axis=0, keepdims=True) for h in range(HEADS)])
        mine_bits.append([jnp.sum(seen[h * 8:h * 8 + 8], axis=0, keepdims=True) for h in range(HEADS)])
    wide = SLOTS * 128
    upper = flag(iota((wide, wide), 0) <= iota((wide, wide), 1))
    lane = iota((1, wide), 1)
    owner = lane & 127
    place = ((owner >> 5) * NX + (owner & 3)) * NZ + ((owner >> 2) & 7)
    place = jnp.broadcast_to(place.astype(jnp.float32), (8, wide))
    slot = jnp.broadcast_to((lane >> 7).astype(jnp.float32), (8, wide))
    sub = iota((8, wide), 0)
    for h in range(HEADS):
        have = jnp.concatenate([mine[s][h] for s in range(SLOTS)], axis=1)
        have_bits = jnp.concatenate([mine_bits[s][h] for s in range(SLOTS)], axis=1)
        have8 = jnp.broadcast_to(have, (8, wide))
        order = jnp.dot(have8.astype(jnp.bfloat16), upper, preferred_element_type=jnp.float32)
        want = (iota((256, wide), 0) + 1).astype(jnp.float32)
        hit = jnp.where((order[0:1, :] == want) & (have > 0), 1.0, 0.0).astype(jnp.bfloat16)
        facts = jnp.where(sub == 0, place, jnp.where(sub == 1, slot, jnp.broadcast_to(have_bits, (8, wide))))
        facts = lax.dot_general(facts.astype(jnp.bfloat16), hit, NT, preferred_element_type=jnp.float32)
        slots_ref[h:h + 1, :] = (facts[0:1, :] * SLOTS + facts[1:2, :]).astype(jnp.int32)
        cubes_ref[h:h + 1, :] = facts[2:3, :].astype(jnp.int32)
        total = jnp.sum(have, axis=1, keepdims=True)
        count_ref[h:h + 1, :] = jnp.broadcast_to(total, (1, 128)).astype(jnp.int32)


def exchange(
    q_hbm, k_hbm, v_hbm, lists_ref, recv, coarse_ref, count_ref, slots_ref, cubes_ref, *scratch
):
    q_own = scratch[0]
    kk = scratch[1:9]
    vv = scratch[9:17]
    (send_buf, tbl_ref, bits_ref, rank_ref, tbl_all, tbl_sm, q_all, pool_k, pool_v, o_res, o_half, o_got, stats, stats_all,
     load_sem, z_send, z_recv, t_send, t_recv, q_send, q_recv, u_send, u_recv,
     o_send, o_recv, m_send, m_recv, sm_sem, loc_sem) = scratch[17:]
    s = lax.axis_index("seq")
    x = lax.rem(s, NX)
    z = lax.rem(lax.div(s, NX), NZ)
    y = lax.div(s, NX * NZ)
    me = y * NX + x

    def peer(j):
        px = lax.rem(x + lax.rem(j, NX), NX)
        py = lax.rem(y + lax.div(j, NX), NY)
        return py * NX + px, (py * NZ + z) * NX + px

    def remote(src, dst, send, recv_, seq):
        return pltpu.make_async_remote_copy(
            src_ref=src, dst_ref=dst, send_sem=send, recv_sem=recv_,
            device_id={"seq": seq}, device_id_type=pl.DeviceIdType.MESH,
        )

    right = (y * NZ + lax.rem(z + 1, NZ)) * NX + x
    left = (y * NZ + lax.rem(z + NZ - 1, NZ)) * NX + x

    loads = []
    for i, (src, dst) in enumerate(((k_hbm, kk[0]), (v_hbm, vv[0]), (q_hbm, q_own))):
        for h in range(HEADS):
            loads.append(pltpu.make_async_copy(
                src.at[:, :, pl.ds(h * HD, HD)], dst.at[pl.ds(h * CUBES, CUBES)], load_sem.at[i * HEADS + h]))
    for c in loads:
        c.start()

    barrier = pltpu.get_barrier_semaphore()
    for seq in (right, left):
        pl.semaphore_signal(barrier, inc=1, device_id={"seq": seq}, device_id_type=pl.DeviceIdType.MESH)

    @pl.loop(1, PLANE)
    def _(j):
        pl.semaphore_signal(barrier, inc=1, device_id={"seq": peer(j)[1]}, device_id_type=pl.DeviceIdType.MESH)

    unit_slots(lists_ref, tbl_ref, bits_ref, rank_ref)
    pl.semaphore_wait(barrier, PLANE + 1)

    @pl.loop(1, PLANE)
    def _(j):
        pp, seq = peer(j)
        remote(tbl_ref, tbl_all.at[me], t_send.at[j], t_recv.at[me], seq).start()

    def ring(first, second, base, far, seq, sem0):
        out = []
        for n in range(14):
            vals = first if n % 4 < 2 else second
            stage = n // 4
            src = vals[0 if stage == 0 else base + stage - 1]
            dst = vals[base + stage if stage < 3 else far]
            part = pl.ds((n % 2) * 24, 24)
            out.append(remote(src.at[part], dst.at[part], z_send.at[sem0 + n], z_recv.at[sem0 + n], seq))
        return out

    to_right = ring(kk, vv, 1, 7, right, 0)
    to_left = ring(vv, kk, 4, 7, left, 14)

    for c in loads[:2 * HEADS]:
        c.wait()
    for n in range(AHEAD):
        to_right[n].start()
        to_left[n].start()

    tbl_all[me] = tbl_ref[...]
    for c in loads[2 * HEADS:]:
        c.wait()

    row = lax.broadcasted_iota(jnp.int32, (CUBES, 512), 0)
    col = lax.broadcasted_iota(jnp.int32, (CUBES, 512), 1)
    mean = jnp.where(lax.div(col, TOK) == row, 1.0 / TOK, 0.0).astype(jnp.bfloat16)

    @pl.loop(0, HEADS)
    def _(h):
        q_all[me, pl.ds(h * CUBES, CUBES), :] = jnp.dot(
            mean, q_own[pl.ds(h * CUBES, CUBES)].reshape(512, HD), preferred_element_type=jnp.float32)

    @pl.loop(1, PLANE)
    def _(j):
        pp, seq = peer(j)
        remote(q_all.at[me], q_all.at[me], q_send.at[j], q_recv.at[me], seq).start()

    @pl.loop(1, PLANE)
    def _(j):
        pp, seq = peer(j)
        remote(tbl_ref, tbl_all.at[pp], t_send.at[j], t_recv.at[pp], seq).wait()

    to_smem = pltpu.make_async_copy(tbl_all, tbl_sm, sm_sem)
    to_smem.start()
    to_smem.wait()

    def owner_z(k):
        if k <= 3:
            return lax.rem(z + NZ - k, NZ)
        if k <= 6:
            return lax.rem(z + k - 3, NZ)
        return lax.rem(z + 4, NZ)

    def pick(k, val, pp):
        lane = (y * NZ + owner_z(k)) * NX + x
        src = vv[k] if val else kk[k]
        for sl in range(SLOTS):
            send_buf[val, k, pp, pl.ds(sl * TOK, TOK), :] = src[jnp.clip(tbl_sm[pp, sl, lane], 0, UNITS - 1)]

    def own_copy(k, val):
        return pltpu.make_async_copy(send_buf.at[val, k, me], recv.at[val, me * NZ + owner_z(k)], loc_sem.at[val, k])

    def handle(k, val):
        oz = owner_z(k)

        @pl.loop(1, PLANE)
        def _(j):
            pp, seq = peer(j)
            pick(k, val, pp)
            remote(send_buf.at[val, k, pp], recv.at[val, me * NZ + oz],
                   u_send.at[val, k, j], u_recv.at[val, oz, me], seq).start()

        if k > 0:
            pick(k, val, me)
            own_copy(k, val).start()

    def pool(k, val):
        src, dst = (vv[k], pool_v) if val else (kk[k], pool_k)

        @pl.loop(0, HEADS)
        def _(h):
            dst[h, pl.ds(k * CUBES, CUBES), :] = jnp.dot(
                mean, src[pl.ds(h * CUBES, CUBES)].reshape(512, HD), preferred_element_type=jnp.float32)

    handle(0, 0)
    handle(0, 1)
    pool(0, 0)
    pool(0, 1)
    head_lists(bits_ref, rank_ref, count_ref, slots_ref, cubes_ref)
    for n in range(14):
        for way in (to_right, to_left):
            way[n].wait_recv()
            if n + AHEAD < 14:
                way[n + AHEAD].start()
        if n % 2:
            stage = n // 4
            val = (n % 4) // 2
            for k, which in ((1 + stage if stage < 3 else 7, val), (4 + stage if stage < 3 else 7, 1 - val)):
                if stage < 3:
                    handle(k, which)
                pool(k, which)

    @pl.loop(1, PLANE)
    def _(j):
        pp, seq = peer(j)
        remote(q_all.at[me], q_all.at[pp], q_send.at[j], q_recv.at[pp], seq).wait()

    lane3 = lax.broadcasted_iota(jnp.int32, (PLANE * CUBES, HD), 1)

    def coarse_head(h, stat):
        rows = pl.ds(pl.multiple_of(h * CUBES, CUBES), CUBES)
        qh = q_all[:, rows, :].reshape(PLANE * CUBES, HD)
        sc = lax.dot_general(qh, pool_k[h], NT, precision=lax.Precision.HIGHEST,
                             preferred_element_type=jnp.float32) * SCALE
        top = jnp.max(sc, axis=1, keepdims=True)
        e = jnp.exp(sc - top)
        tot = jnp.sum(e, axis=1, keepdims=True)
        o = jnp.dot(e, pool_v[h], precision=lax.Precision.HIGHEST, preferred_element_type=jnp.float32)
        o_res[:, rows, :] = o.reshape(PLANE, CUBES, HD)
        stat = jnp.where(lane3 == h, top, stat)
        return jnp.where(lane3 == h + 64, tot, stat)

    stat = lax.fori_loop(0, HEADS, coarse_head, jnp.zeros((PLANE * CUBES, HD), jnp.float32))
    stats[...] = stat.reshape(PLANE, CUBES, HD)
    o_half[...] = o_res[...].astype(jnp.bfloat16)

    @pl.loop(1, PLANE)
    def _(j):
        pp, seq = peer(j)
        remote(o_half.at[pp], o_got.at[me], o_send.at[j], o_recv.at[me], seq).start()
        remote(stats.at[pp], stats_all.at[me], m_send.at[j], m_recv.at[me], seq).start()

    handle(7, 0)
    handle(7, 1)
    o_got[me] = o_half[me]
    stats_all[me] = stats[me]

    @pl.loop(1, PLANE)
    def _(j):
        pp, seq = peer(j)
        remote(o_half.at[pp], o_got.at[pp], o_send.at[j], o_recv.at[pp], seq).wait()
        remote(stats.at[pp], stats_all.at[pp], m_send.at[j], m_recv.at[pp], seq).wait()

    o_res[...] = o_got[...].astype(jnp.float32)
    for h in range(HEADS):
        top = stats_all[:, :, h:h + 1]
        tot = stats_all[:, :, 64 + h:65 + h]
        w = jnp.exp(top - jnp.max(top, axis=0, keepdims=True))
        den = jnp.sum(w * tot, axis=0)
        num = jnp.sum(w * o_res[:, pl.ds(h * CUBES, CUBES), :], axis=0)
        coarse_ref[pl.ds(h * CUBES, CUBES), :] = num / den

    for c in to_right + to_left:
        c.wait_send()
    for k in range(NZ):
        oz = owner_z(k)
        for val in range(2):
            if k > 0:
                own_copy(k, val).wait()

            @pl.loop(1, PLANE)
            def _(j):
                pp, seq = peer(j)
                remote(send_buf.at[val, k, pp], recv.at[val, pp * NZ + oz],
                       u_send.at[val, k, j], u_recv.at[val, oz, pp], seq).wait()


def fine(count_ref, slot_ref, bits_ref, gate_ref, q_ref, k_ref, v_ref, coarse_ref, recv_hbm, out_ref,
         recv, s_buf, s_own, top, peak, tot, acc, sem):
    c2 = SCALE * LOG2E
    pairs = GROUP // 2
    copies = [pltpu.make_async_copy(recv_hbm.at[i], recv.at[i], sem.at[i]) for i in range(2)]
    for c in copies:
        c.start()
    same = (lax.broadcasted_iota(jnp.int32, (128, 128), 0) < TOK) == (
        lax.broadcasted_iota(jnp.int32, (128, 128), 1) < TOK)
    lane = lax.broadcasted_iota(jnp.int32, (1, 128), 1)

    def columns(h):
        return pl.ds(pl.multiple_of(h * HD, HD), HD)

    def blocks(h):
        return lax.div(count_ref[jnp.minimum(h, HEADS - 1), 0] + GROUP - 1, GROUP)

    def step(at):
        h, g = at
        last = g + 1 >= blocks(h)
        return jnp.where(last, h + 1, h), jnp.where(last, 0, g + 1)

    def units(val, h, g):
        return jnp.concatenate(
            [recv[val, slot_ref[h, jnp.minimum(g * GROUP + t, count_ref[h, 0] - 1)]] for t in range(GROUP)], axis=0)

    def score(i, at):
        h, g = at
        slot = lax.rem(i, RING)
        sc = lax.dot_general(q_ref[:, columns(h)], units(0, h, g), NT, preferred_element_type=jnp.float32)
        rowbits = [
            jnp.where(lane < TOK, bits_ref[h, g * GROUP + 2 * t], bits_ref[h, g * GROUP + 2 * t + 1])
            for t in range(pairs)
        ]
        for c in range(CUBES):
            rows = pl.ds(c * TOK, TOK)
            best = top[h, rows, :]
            for t in range(pairs):
                bias = jnp.where((rowbits[t] >> c) & 1 == 1, 0.0, NEG)
                part = sc[c * TOK:(c + 1) * TOK, t * 128:(t + 1) * 128] + bias
                s_buf[slot, t, rows, :] = part
                best = jnp.maximum(best, part)
            top[h, rows, :] = best

    def begin(at):
        h, g = at

        @pl.when(g == 0)
        def _():
            peak[...] = jnp.broadcast_to(jnp.max(top[h], axis=1, keepdims=True) * c2, (CUBES * TOK, HD))
            for c in range(CUBES // 2):
                rows = pl.ds(c * 128, 128)
                e = jnp.exp2(s_own[h, rows, :] * c2 - peak[rows, :])
                tot[rows, :] = e
                acc[rows, :] = jnp.dot(
                    e.astype(jnp.bfloat16), v_ref[rows, columns(h)], preferred_element_type=jnp.float32)

    def value(i, at):
        h, g = at
        slot = lax.rem(i, RING)
        blocks_of_rows = []
        for c in range(CUBES):
            rows = pl.ds(c * TOK, TOK)
            high, sums, parts = peak[rows, :], tot[rows, :], []
            for t in range(pairs):
                e = jnp.exp2(s_buf[slot, t, rows, :] * c2 - high)
                sums += e
                parts.append(e.astype(jnp.bfloat16))
            tot[rows, :] = sums
            blocks_of_rows.append(jnp.concatenate(parts, axis=1))
        acc[...] += jnp.dot(
            jnp.concatenate(blocks_of_rows, axis=0), units(1, h, g), preferred_element_type=jnp.float32)

    def finish(at):
        h, g = at

        @pl.when(g + 1 == blocks(h))
        def _():
            for c in range(CUBES):
                rows = pl.ds(c * TOK, TOK)
                total = jnp.sum(tot[rows, :], axis=1, keepdims=True)
                pooled = gate_ref[h] * coarse_ref[pl.ds(h * CUBES + c, 1), :]
                out_ref[rows, columns(h)] = (acc[rows, :] / total + pooled).astype(jnp.bfloat16)

    @pl.loop(0, HEADS)
    def _(h):
        for c in range(CUBES // 2):
            rows = pl.ds(c * 128, 128)
            sc = lax.dot_general(
                q_ref[rows, columns(h)], k_ref[rows, columns(h)], NT, preferred_element_type=jnp.float32)
            sc = jnp.where(same, sc, NEG)
            s_own[h, rows, :] = sc
            top[h, rows, :] = sc

    longest, items = blocks(0), blocks(0)
    for h in range(1, HEADS):
        longest, items = jnp.maximum(longest, blocks(h)), items + blocks(h)
    copies[0].wait()

    def only_score(i, at):
        score(i, at)
        return step(at)

    def both(i, carry):
        ahead, at = carry
        begin(at)
        value(i - longest, at)
        score(i, ahead)
        finish(at)
        return step(ahead), step(at)

    def only_value(i, at):
        begin(at)
        value(i - longest, at)
        finish(at)
        return step(at)

    zero = jnp.int32(0)
    ahead = lax.fori_loop(0, longest, only_score, (zero, zero))
    copies[1].wait()
    ahead, at = lax.fori_loop(longest, items, both, (ahead, (zero, zero)))
    lax.fori_loop(items, items + longest, only_value, at)


def project(att_ref, w_hbm, out_ref, other, w_buf, total, send_sem, recv_sem, w_sem):
    head = lax.axis_index("head")
    width = HEADS * HD
    weights = pltpu.make_async_copy(w_hbm.at[:, pl.ds(pl.multiple_of(head * width, width), width)], w_buf, w_sem)
    weights.start()
    barrier = pltpu.get_barrier_semaphore()
    pl.semaphore_signal(barrier, inc=1, device_id={"head": 1 - head}, device_id_type=pl.DeviceIdType.MESH)
    pl.semaphore_wait(barrier, 1)
    swap = pltpu.make_async_remote_copy(
        src_ref=att_ref, dst_ref=other, send_sem=send_sem, recv_sem=recv_sem,
        device_id={"head": 1 - head}, device_id_type=pl.DeviceIdType.MESH)
    swap.start()
    weights.wait()
    mine = pl.ds(pl.multiple_of(head * width, width), width)
    theirs = pl.ds(pl.multiple_of((1 - head) * width, width), width)
    total[...] = jnp.dot(att_ref[...], w_buf[mine, :], preferred_element_type=jnp.float32)
    swap.wait()
    out_ref[...] = (
        total[...] + jnp.dot(other[...], w_buf[theirs, :], preferred_element_type=jnp.float32)).astype(jnp.bfloat16)


def body(query_input, key_input, value_input, cube_lists, coarse_gate, out_weight):
    lists = jnp.transpose(cube_lists, (1, 0, 2)).reshape(HEADS, CUBES * TOP)
    any_spec = pl.BlockSpec(memory_space=pl.ANY)
    vmem_spec = pl.BlockSpec(memory_space=pltpu.VMEM)
    smem_spec = pl.BlockSpec(memory_space=pltpu.SMEM)
    dma = pltpu.SemaphoreType.DMA
    recv, coarse, count, slots, cubes = pl.pallas_call(
        exchange,
        out_shape=(
            jax.ShapeDtypeStruct((2, PLANE * NZ, PACK, HD), jnp.bfloat16),
            jax.ShapeDtypeStruct((UNITS, HD), jnp.float32),
            jax.ShapeDtypeStruct((HEADS, 128), jnp.int32),
            jax.ShapeDtypeStruct((HEADS, 256), jnp.int32),
            jax.ShapeDtypeStruct((HEADS, 256), jnp.int32),
        ),
        in_specs=[any_spec] * 3 + [vmem_spec],
        out_specs=(any_spec,) + (vmem_spec,) * 4,
        scratch_shapes=[pltpu.VMEM((UNITS, TOK, HD), jnp.bfloat16)] * 17 + [
            pltpu.VMEM((2, NZ, PLANE, PACK, HD), jnp.bfloat16),
            pltpu.VMEM((8, 128), jnp.int32),
            pltpu.VMEM((UNITS, 128), jnp.float32),
            pltpu.VMEM((UNITS, 128), jnp.float32),
            pltpu.VMEM((PLANE, 8, 128), jnp.int32),
            pltpu.SMEM((PLANE, 8, 128), jnp.int32),
            pltpu.VMEM((PLANE, UNITS, HD), jnp.float32),
            pltpu.VMEM((HEADS, NZ * CUBES, HD), jnp.float32),
            pltpu.VMEM((HEADS, NZ * CUBES, HD), jnp.float32),
            pltpu.VMEM((PLANE, UNITS, HD), jnp.float32),
            pltpu.VMEM((PLANE, UNITS, HD), jnp.bfloat16),
            pltpu.VMEM((PLANE, UNITS, HD), jnp.bfloat16),
            pltpu.VMEM((PLANE, CUBES, HD), jnp.float32),
            pltpu.VMEM((PLANE, CUBES, HD), jnp.float32),
            dma((18,)), dma((28,)), dma((28,)), dma((PLANE,)), dma((PLANE,)), dma((PLANE,)), dma((PLANE,)),
            dma((2, NZ, PLANE)), dma((2, NZ, PLANE)), dma((PLANE,)), dma((PLANE,)), dma((PLANE,)), dma((PLANE,)), dma, dma((2, NZ)),
        ],
        compiler_params=pltpu.CompilerParams(
            collective_id=0, has_side_effects=True, vmem_limit_bytes=56 * 1024 * 1024),
        name="exchange",
    )(*[t.reshape(CUBES, TOK, HEADS * HD) for t in (query_input, key_input, value_input)], lists)
    attended = pl.pallas_call(
        fine,
        out_shape=jax.ShapeDtypeStruct((CUBES * TOK, HEADS * HD), jnp.bfloat16),
        in_specs=[smem_spec] * 4 + [vmem_spec] * 4 + [any_spec],
        out_specs=vmem_spec,
        scratch_shapes=[
            pltpu.VMEM((2, PLANE * NZ * SLOTS, TOK, HD), jnp.bfloat16),
            pltpu.VMEM((RING, GROUP // 2, CUBES * TOK, HD), jnp.float32),
        ] + [pltpu.VMEM((HEADS, CUBES * TOK, HD), jnp.float32)] * 2 + [pltpu.VMEM((CUBES * TOK, HD), jnp.float32)] * 3
        + [dma((2,))],
        compiler_params=pltpu.CompilerParams(vmem_limit_bytes=56 * 1024 * 1024),
        name="fine",
    )(count, slots, cubes, coarse_gate, query_input, key_input, value_input, coarse,
      recv.reshape(2, PLANE * NZ * SLOTS, TOK, HD))
    shape = (CUBES * TOK, HEADS * HD)
    return pl.pallas_call(
        project,
        out_shape=jax.ShapeDtypeStruct(shape, jnp.bfloat16),
        in_specs=[vmem_spec, any_spec],
        out_specs=vmem_spec,
        scratch_shapes=[
            pltpu.VMEM(shape, jnp.bfloat16),
            pltpu.VMEM((2 * HEADS * HD, HEADS * HD), jnp.bfloat16),
            pltpu.VMEM(shape, jnp.float32),
            dma, dma, dma,
        ],
        compiler_params=pltpu.CompilerParams(
            collective_id=1, has_side_effects=True, vmem_limit_bytes=60 * 1024 * 1024),
        name="project",
    )(attended, out_weight)


def solution(mesh):
    placed = (
        P("seq", "head"),
        P("seq", "head"),
        P("seq", "head"),
        P("seq", "head", None),
        P("head"),
        P(),
    )
    return jax.shard_map(
        body, mesh=mesh, in_specs=placed, out_specs=P("seq", "head"), check_vma=False
    )
```

```python
import functools

import jax
import jax.numpy as jnp
from jax import lax
from jax.experimental import pallas as pl
from jax.experimental.pallas import tpu as pltpu
from jax.sharding import PartitionSpec as P

NX, NY, NZ = 4, 4, 8
PLANE = NX * NY
SLOTS = 3
CUBES = 8
HEADS = 6
TOK = 64
HD = 128
TOP = 32
UNITS = CUBES * HEADS
MAXU = 144
GROUP = 8
RING = MAXU // GROUP
NEG = -1e30
AHEAD = 4
EARLY = {0: 0, 1: 1, 2: 2, 4: 3, 5: 4}
LATE = {3: 0, 6: 1, 7: 2}
SAFE = PLANE * SLOTS
SCALE = HD ** -0.5
LOG2E = 1.4426950408889634
NT = (((1,), (1,)), ((), ()))


def iota(shape, dim):
    return lax.broadcasted_iota(jnp.int32, shape, dim)


def flag(mask):
    return jnp.where(mask, 1.0, 0.0).astype(jnp.bfloat16)


def unit_slots(z, lists_ref, table_ref, bits_ref, rank_ref, pos_ref):
    entry_bit = 1 << (iota((CUBES, 256), 1) >> 5)
    bits, hots = [], []
    for h in range(HEADS):
        row = lists_ref[h:h + 1, :]
        owner_hot = flag((row >> 3) == iota((128, 256), 0))
        hots.append(owner_hot)
        within_bit = jnp.where((row & 7) == iota((CUBES, 256), 0), entry_bit, 0)
        bits.append(lax.dot_general(within_bit.astype(jnp.float32).astype(jnp.bfloat16), owner_hot, NT,
                                    preferred_element_type=jnp.float32))
    bits = jnp.concatenate(bits, axis=0)
    need = bits > 0
    lower = flag(iota((UNITS, UNITS), 0) >= iota((UNITS, UNITS), 1))
    rank = jnp.dot(lower, flag(need), preferred_element_type=jnp.float32)
    bits_ref[...] = bits
    rank_ref[...] = rank
    unit = iota((UNITS, 128), 0)
    table_ref[...] = jnp.zeros_like(table_ref)
    for s in range(SLOTS):
        table_ref[s:s + 1, :] = jnp.sum(jnp.where(need & (rank == s + 1), unit, 0), axis=0, keepdims=True)
    pos_ref[...] = jnp.zeros_like(pos_ref)
    for h in range(HEADS):
        row = lists_ref[h:h + 1, :]
        owner = row >> 3
        spread = jnp.dot(rank[h * 8:h * 8 + 8].astype(jnp.bfloat16), hots[h], preferred_element_type=jnp.float32)
        here = jnp.where((row & 7) == iota((CUBES, 256), 0), spread, 0.0)
        order = jnp.sum(here, axis=0, keepdims=True).astype(jnp.int32) - 1
        ahead = (((owner >> 2) & 7) - z) & 7
        which = jnp.where(ahead == 0, 0, jnp.where(ahead >= 6, 8 - ahead, ahead + 2))
        column = (owner >> 5) * NX + (owner & 3)
        late = (ahead >= 3) & (ahead <= 5)
        pos_ref[h:h + 1, :] = jnp.where(late, -1, (which * PLANE + column) * SLOTS + order)


def head_lists(z, bits_ref, rank_ref, count_ref, slots_ref, cubes_ref):
    bits, rank = bits_ref[...], rank_ref[...]
    need = bits > 0
    ahead = (((iota((UNITS, 128), 1) >> 2) & 7) - z) & 7
    late = (ahead >= 3) & (ahead <= 5)
    mine, mine_bits = [], []
    for s in range(SLOTS):
        hit = jnp.where(need & (rank == s + 1) & late, 1.0, 0.0)
        seen = hit * bits
        mine.append([jnp.sum(hit[h * 8:h * 8 + 8], axis=0, keepdims=True) for h in range(HEADS)])
        mine_bits.append([jnp.sum(seen[h * 8:h * 8 + 8], axis=0, keepdims=True) for h in range(HEADS)])
    wide = SLOTS * 128
    upper = flag(iota((wide, wide), 0) <= iota((wide, wide), 1))
    lane = iota((1, wide), 1)
    owner = lane & 127
    ahead = (((owner >> 2) & 7) - z) & 7
    index = jnp.where(ahead == 5, 0, jnp.where(ahead == 3, 1, 2))
    place = ((owner >> 5) * NX + (owner & 3)) * len(LATE) + index
    place = jnp.broadcast_to(place.astype(jnp.float32), (8, wide))
    slot = jnp.broadcast_to((lane >> 7).astype(jnp.float32), (8, wide))
    sub = iota((8, wide), 0)
    for h in range(HEADS):
        have = jnp.concatenate([mine[s][h] for s in range(SLOTS)], axis=1)
        have_bits = jnp.concatenate([mine_bits[s][h] for s in range(SLOTS)], axis=1)
        have8 = jnp.broadcast_to(have, (8, wide))
        order = jnp.dot(have8.astype(jnp.bfloat16), upper, preferred_element_type=jnp.float32)
        want = (iota((256, wide), 0) + 1).astype(jnp.float32)
        hit = jnp.where((order[0:1, :] == want) & (have > 0), 1.0, 0.0).astype(jnp.bfloat16)
        facts = jnp.where(sub == 0, place, jnp.where(sub == 1, slot, jnp.broadcast_to(have_bits, (8, wide))))
        facts = lax.dot_general(facts.astype(jnp.bfloat16), hit, NT, preferred_element_type=jnp.float32)
        slots_ref[h:h + 1, :] = (facts[0:1, :] * SLOTS + facts[1:2, :]).astype(jnp.int32)
        cubes_ref[h:h + 1, :] = facts[2:3, :].astype(jnp.int32)
        total = jnp.sum(have, axis=1, keepdims=True)
        count_ref[h:h + 1, :] = jnp.broadcast_to(total, (1, 128)).astype(jnp.int32)


def exchange(
    q_hbm, k_hbm, v_hbm, lists_ref, recv, coarse_ref, count_ref, slots_ref, cubes_ref, part_ref, stat_ref, *scratch
):
    q_own = scratch[0]
    kk = scratch[1:9]
    vv = scratch[9:17]
    (send_buf, early, tbl_ref, bits_ref, rank_ref, pos_ref, pos_sm, tbl_all, tbl_sm, q_all, pool_k, pool_v, o_res, o_half, o_got, stats, stats_all,
     load_sem, z_send, z_recv, t_send, t_recv, q_send, q_recv, u_send, u_recv,
     o_send, o_recv, m_send, m_recv, sm_sem, pos_sem, loc_sem) = scratch[17:]
    s = lax.axis_index("seq")
    x = lax.rem(s, NX)
    z = lax.rem(lax.div(s, NX), NZ)
    y = lax.div(s, NX * NZ)
    me = y * NX + x

    def peer(j):
        px = lax.rem(x + lax.rem(j, NX), NX)
        py = lax.rem(y + lax.div(j, NX), NY)
        return py * NX + px, (py * NZ + z) * NX + px

    def remote(src, dst, send, recv_, seq):
        return pltpu.make_async_remote_copy(
            src_ref=src, dst_ref=dst, send_sem=send, recv_sem=recv_,
            device_id={"seq": seq}, device_id_type=pl.DeviceIdType.MESH,
        )

    right = (y * NZ + lax.rem(z + 1, NZ)) * NX + x
    left = (y * NZ + lax.rem(z + NZ - 1, NZ)) * NX + x

    loads = []
    for i, (src, dst) in enumerate(((k_hbm, kk[0]), (v_hbm, vv[0]), (q_hbm, q_own))):
        for h in range(HEADS):
            loads.append(pltpu.make_async_copy(
                src.at[:, :, pl.ds(h * HD, HD)], dst.at[pl.ds(h * CUBES, CUBES)], load_sem.at[i * HEADS + h]))
    for c in loads:
        c.start()

    barrier = pltpu.get_barrier_semaphore()
    for seq in (right, left):
        pl.semaphore_signal(barrier, inc=1, device_id={"seq": seq}, device_id_type=pl.DeviceIdType.MESH)

    @pl.loop(1, PLANE)
    def _(j):
        pl.semaphore_signal(barrier, inc=1, device_id={"seq": peer(j)[1]}, device_id_type=pl.DeviceIdType.MESH)

    unit_slots(z, lists_ref, tbl_ref, bits_ref, rank_ref, pos_ref)
    pl.semaphore_wait(barrier, PLANE + 1)

    @pl.loop(1, PLANE)
    def _(j):
        pp, seq = peer(j)
        remote(tbl_ref, tbl_all.at[me], t_send.at[j], t_recv.at[me], seq).start()

    def ring(first, second, base, far, seq, sem0):
        out = []
        for n in range(14):
            vals = first if n % 4 < 2 else second
            stage = n // 4
            src = vals[0 if stage == 0 else base + stage - 1]
            dst = vals[base + stage if stage < 3 else far]
            part = pl.ds((n % 2) * 24, 24)
            out.append(remote(src.at[part], dst.at[part], z_send.at[sem0 + n], z_recv.at[sem0 + n], seq))
        return out

    to_right = ring(kk, vv, 1, 7, right, 0)
    to_left = ring(vv, kk, 4, 7, left, 14)

    for c in loads[:2 * HEADS]:
        c.wait()
    for n in range(AHEAD):
        to_right[n].start()
        to_left[n].start()

    tbl_all[me] = tbl_ref[...]
    for c in loads[2 * HEADS:]:
        c.wait()

    row = lax.broadcasted_iota(jnp.int32, (CUBES, 512), 0)
    col = lax.broadcasted_iota(jnp.int32, (CUBES, 512), 1)
    mean = jnp.where(lax.div(col, TOK) == row, 1.0 / TOK, 0.0).astype(jnp.bfloat16)

    @pl.loop(0, HEADS)
    def _(h):
        q_all[me, pl.ds(h * CUBES, CUBES), :] = jnp.dot(
            mean, q_own[pl.ds(h * CUBES, CUBES)].reshape(512, HD), preferred_element_type=jnp.float32)

    @pl.loop(1, PLANE)
    def _(j):
        pp, seq = peer(j)
        remote(q_all.at[me], q_all.at[me], q_send.at[j], q_recv.at[me], seq).start()

    @pl.loop(1, PLANE)
    def _(j):
        pp, seq = peer(j)
        remote(tbl_ref, tbl_all.at[pp], t_send.at[j], t_recv.at[pp], seq).wait()

    to_smem_pos = pltpu.make_async_copy(pos_ref, pos_sm, pos_sem)
    to_smem_pos.start()
    to_smem = pltpu.make_async_copy(tbl_all, tbl_sm, sm_sem)
    to_smem.start()
    to_smem.wait()
    to_smem_pos.wait()

    def owner_z(k):
        if k <= 3:
            return lax.rem(z + NZ - k, NZ)
        if k <= 6:
            return lax.rem(z + k - 3, NZ)
        return lax.rem(z + 4, NZ)

    def unit_of(k, val, pp, sl):
        lane = (y * NZ + owner_z(k)) * NX + x
        return (vv[k] if val else kk[k])[jnp.clip(tbl_sm[pp, sl, lane], 0, UNITS - 1)]

    def landing(k, val, p):
        if k in EARLY:
            return early.at[val, pl.ds((EARLY[k] * PLANE + p) * SLOTS, SLOTS)]
        return recv.at[val, pl.ds((p * len(LATE) + LATE[k]) * SLOTS, SLOTS)]

    def own_copy(k, val):
        return pltpu.make_async_copy(send_buf.at[val, k, me], landing(k, val, me), loc_sem.at[val, LATE[k]])

    def handle(k, val):
        @pl.loop(1, PLANE)
        def _(j):
            pp, seq = peer(j)
            for sl in range(SLOTS):
                send_buf[val, k, pp, sl] = unit_of(k, val, pp, sl)
            remote(send_buf.at[val, k, pp], landing(k, val, me), u_send.at[val, k, j], u_recv.at[val, k, me], seq).start()

        for sl in range(SLOTS):
            if k in LATE:
                send_buf[val, k, me, sl] = unit_of(k, val, me, sl)
            elif k > 0:
                early[val, (EARLY[k] * PLANE + me) * SLOTS + sl] = unit_of(k, val, me, sl)
        if k in LATE:
            own_copy(k, val).start()

    def arrived(k, val):
        @pl.loop(1, PLANE)
        def _(j):
            pp, seq = peer(j)
            remote(send_buf.at[val, k, pp], landing(k, val, pp), u_send.at[val, k, j], u_recv.at[val, k, pp], seq).wait_recv()

    low_lanes = iota((1, 128), 1) < TOK

    def attend(i):
        h, c = lax.div(i, CUBES), lax.rem(i, CUBES)
        q = q_own[i]
        scores = [lax.dot_general(q, kk[0][i], NT, preferred_element_type=jnp.float32)]
        spots = [pos_sm[h, c * TOP + t] for t in range(TOP)]
        where = [jnp.clip(jnp.where(p < 0, SAFE, p), 0, len(EARLY) * PLANE * SLOTS - 1) for p in spots]
        bias = [jnp.where(p < 0, NEG, 0.0) for p in spots]
        for g in range(TOP // 4):
            keys = jnp.concatenate([early[0, where[4 * g + t]] for t in range(4)], axis=0)
            sc = lax.dot_general(q, keys, NT, preferred_element_type=jnp.float32)
            hide = jnp.concatenate(
                [jnp.where(low_lanes, bias[4 * g + t], bias[4 * g + t + 1]) for t in (0, 2)], axis=1)
            scores.append(sc + hide)
        top = functools.reduce(jnp.maximum, scores[1:])
        top = jnp.maximum(jnp.max(top, axis=1, keepdims=True), jnp.max(scores[0], axis=1, keepdims=True))
        es = [jnp.exp2((sc - top) * (SCALE * LOG2E)) for sc in scores]
        tot = jnp.sum(es[0], axis=1, keepdims=True) + jnp.sum(sum(es[2:], es[1]), axis=1, keepdims=True)
        acc = jnp.dot(es[0].astype(jnp.bfloat16), vv[0][i], preferred_element_type=jnp.float32)
        for g in range(TOP // 4):
            vals = jnp.concatenate([early[1, where[4 * g + t]] for t in range(4)], axis=0)
            acc += jnp.dot(es[g + 1].astype(jnp.bfloat16), vals, preferred_element_type=jnp.float32)
        part_ref[i] = acc
        stat_ref[i] = jnp.where(low_lanes, top, tot)

    def attend_range(lo, hi):
        @pl.loop(lo, hi)
        def _(i):
            attend(i)

    def pool(k, val):
        src, dst = (vv[k], pool_v) if val else (kk[k], pool_k)

        @pl.loop(0, HEADS)
        def _(h):
            dst[h, pl.ds(k * CUBES, CUBES), :] = jnp.dot(
                mean, src[pl.ds(h * CUBES, CUBES)].reshape(512, HD), preferred_element_type=jnp.float32)

    handle(0, 0)
    handle(0, 1)
    pool(0, 0)
    pool(0, 1)
    head_lists(z, bits_ref, rank_ref, count_ref, slots_ref, cubes_ref)
    for n in range(14):
        for way in (to_right, to_left):
            way[n].wait_recv()
            if n + AHEAD < 14:
                way[n + AHEAD].start()
        if n % 2:
            stage = n // 4
            val = (n % 4) // 2
            for k, which in ((1 + stage if stage < 3 else 7, val), (4 + stage if stage < 3 else 7, 1 - val)):
                if stage < 3:
                    handle(k, which)
                pool(k, which)
        if n == 10:
            for k in EARLY:
                arrived(k, 0)
                arrived(k, 1)
            attend_range(0, 8)
        if n == 11:
            attend_range(8, 22)
        if n == 12:
            attend_range(22, 30)

    @pl.loop(1, PLANE)
    def _(j):
        pp, seq = peer(j)
        remote(q_all.at[me], q_all.at[pp], q_send.at[j], q_recv.at[pp], seq).wait()

    lane3 = lax.broadcasted_iota(jnp.int32, (PLANE * CUBES, HD), 1)

    def coarse_head(h, stat):
        rows = pl.ds(pl.multiple_of(h * CUBES, CUBES), CUBES)
        qh = q_all[:, rows, :].reshape(PLANE * CUBES, HD)
        sc = lax.dot_general(qh, pool_k[h], NT, precision=lax.Precision.HIGHEST,
                             preferred_element_type=jnp.float32) * SCALE
        top = jnp.max(sc, axis=1, keepdims=True)
        e = jnp.exp(sc - top)
        tot = jnp.sum(e, axis=1, keepdims=True)
        o = jnp.dot(e, pool_v[h], precision=lax.Precision.HIGHEST, preferred_element_type=jnp.float32)
        o_res[:, rows, :] = o.reshape(PLANE, CUBES, HD)
        stat = jnp.where(lane3 == h, top, stat)
        return jnp.where(lane3 == h + 64, tot, stat)

    stat = lax.fori_loop(0, HEADS, coarse_head, jnp.zeros((PLANE * CUBES, HD), jnp.float32))
    stats[...] = stat.reshape(PLANE, CUBES, HD)
    o_half[...] = o_res[...].astype(jnp.bfloat16)

    @pl.loop(1, PLANE)
    def _(j):
        pp, seq = peer(j)
        remote(o_half.at[pp], o_got.at[me], o_send.at[j], o_recv.at[me], seq).start()
        remote(stats.at[pp], stats_all.at[me], m_send.at[j], m_recv.at[me], seq).start()

    handle(7, 0)
    handle(7, 1)
    attend_range(30, UNITS)
    o_got[me] = o_half[me]
    stats_all[me] = stats[me]

    @pl.loop(1, PLANE)
    def _(j):
        pp, seq = peer(j)
        remote(o_half.at[pp], o_got.at[pp], o_send.at[j], o_recv.at[pp], seq).wait()
        remote(stats.at[pp], stats_all.at[pp], m_send.at[j], m_recv.at[pp], seq).wait()

    o_res[...] = o_got[...].astype(jnp.float32)
    for h in range(HEADS):
        top = stats_all[:, :, h:h + 1]
        tot = stats_all[:, :, 64 + h:65 + h]
        w = jnp.exp(top - jnp.max(top, axis=0, keepdims=True))
        den = jnp.sum(w * tot, axis=0)
        num = jnp.sum(w * o_res[:, pl.ds(h * CUBES, CUBES), :], axis=0)
        coarse_ref[pl.ds(h * CUBES, CUBES), :] = num / den

    for c in to_right + to_left:
        c.wait_send()
    for k in range(NZ):
        for val in range(2):
            if k in LATE:
                own_copy(k, val).wait()
                arrived(k, val)

            @pl.loop(1, PLANE)
            def _(j):
                pp, seq = peer(j)
                remote(send_buf.at[val, k, pp], landing(k, val, me), u_send.at[val, k, j], u_recv.at[val, k, me], seq).wait_send()


def fine(count_ref, slot_ref, bits_ref, gate_ref, q_ref, part_ref, stat_ref, coarse_ref, recv_hbm, out_ref,
         recv, s_buf, top, peak, tot, acc, sem):
    c2 = SCALE * LOG2E
    pairs = GROUP // 2
    copies = [pltpu.make_async_copy(recv_hbm.at[i], recv.at[i], sem.at[i]) for i in range(2)]
    for c in copies:
        c.start()
    lane = lax.broadcasted_iota(jnp.int32, (1, 128), 1)

    def columns(h):
        return pl.ds(pl.multiple_of(h * HD, HD), HD)

    def blocks(h):
        return jnp.maximum(lax.div(count_ref[jnp.minimum(h, HEADS - 1), 0] + GROUP - 1, GROUP), 1)

    def step(at):
        h, g = at
        last = g + 1 >= blocks(h)
        return jnp.where(last, h + 1, h), jnp.where(last, 0, g + 1)

    def units(val, h, g):
        return jnp.concatenate(
            [recv[val, slot_ref[h, jnp.clip(count_ref[h, 0] - 1, 0, g * GROUP + t)]] for t in range(GROUP)], axis=0)

    def score(i, at):
        h, g = at
        slot = lax.rem(i, RING)
        sc = lax.dot_general(q_ref[:, columns(h)], units(0, h, g), NT, preferred_element_type=jnp.float32)
        rowbits = [
            jnp.where(lane < TOK, bits_ref[h, g * GROUP + 2 * t], bits_ref[h, g * GROUP + 2 * t + 1])
            for t in range(pairs)
        ]
        for c in range(CUBES):
            rows = pl.ds(c * TOK, TOK)
            best = top[h, rows, :]
            for t in range(pairs):
                bias = jnp.where((rowbits[t] >> c) & 1 == 1, 0.0, NEG)
                part = sc[c * TOK:(c + 1) * TOK, t * 128:(t + 1) * 128] + bias
                s_buf[slot, t, rows, :] = part
                best = jnp.maximum(best, part)
            top[h, rows, :] = best

    def begin(at):
        h, g = at

        @pl.when(g == 0)
        def _():
            peak[...] = jnp.broadcast_to(jnp.max(top[h], axis=1, keepdims=True) * c2, (CUBES * TOK, HD))
            for c in range(CUBES):
                rows = pl.ds(c * TOK, TOK)
                state = stat_ref[h * CUBES + c]
                shrink = jnp.exp2(state[:, 0:1] * c2 - peak[rows, :])
                tot[rows, :] = shrink * (state[:, TOK:TOK + 1] * (1.0 / HD))
                acc[rows, :] = shrink * part_ref[h * CUBES + c]

    def value(i, at):
        h, g = at
        slot = lax.rem(i, RING)
        blocks_of_rows = []
        for c in range(CUBES):
            rows = pl.ds(c * TOK, TOK)
            high, sums, parts = peak[rows, :], tot[rows, :], []
            for t in range(pairs):
                e = jnp.exp2(s_buf[slot, t, rows, :] * c2 - high)
                sums += e
                parts.append(e.astype(jnp.bfloat16))
            tot[rows, :] = sums
            blocks_of_rows.append(jnp.concatenate(parts, axis=1))
        acc[...] += jnp.dot(
            jnp.concatenate(blocks_of_rows, axis=0), units(1, h, g), preferred_element_type=jnp.float32)

    def finish(at):
        h, g = at

        @pl.when(g + 1 == blocks(h))
        def _():
            for c in range(CUBES):
                rows = pl.ds(c * TOK, TOK)
                total = jnp.sum(tot[rows, :], axis=1, keepdims=True)
                pooled = gate_ref[h] * coarse_ref[pl.ds(h * CUBES + c, 1), :]
                out_ref[rows, columns(h)] = (acc[rows, :] / total + pooled).astype(jnp.bfloat16)

    @pl.loop(0, UNITS)
    def _(i):
        top[lax.div(i, CUBES), pl.ds(pl.multiple_of(lax.rem(i, CUBES) * TOK, TOK), TOK), :] = jnp.broadcast_to(
            stat_ref[i][:, 0:1], (TOK, HD))

    longest, items = blocks(0), blocks(0)
    for h in range(1, HEADS):
        longest, items = jnp.maximum(longest, blocks(h)), items + blocks(h)
    copies[0].wait()

    def only_score(i, at):
        score(i, at)
        return step(at)

    def both(i, carry):
        ahead, at = carry
        begin(at)
        value(i - longest, at)
        score(i, ahead)
        finish(at)
        return step(ahead), step(at)

    def only_value(i, at):
        begin(at)
        value(i - longest, at)
        finish(at)
        return step(at)

    zero = jnp.int32(0)
    ahead = lax.fori_loop(0, longest, only_score, (zero, zero))
    copies[1].wait()
    ahead, at = lax.fori_loop(longest, items, both, (ahead, (zero, zero)))
    lax.fori_loop(items, items + longest, only_value, at)


def project(att_ref, w_hbm, out_ref, other, w_buf, total, send_sem, recv_sem, w_sem):
    head = lax.axis_index("head")
    width = HEADS * HD
    weights = pltpu.make_async_copy(w_hbm.at[:, pl.ds(pl.multiple_of(head * width, width), width)], w_buf, w_sem)
    weights.start()
    barrier = pltpu.get_barrier_semaphore()
    pl.semaphore_signal(barrier, inc=1, device_id={"head": 1 - head}, device_id_type=pl.DeviceIdType.MESH)
    pl.semaphore_wait(barrier, 1)
    swap = pltpu.make_async_remote_copy(
        src_ref=att_ref, dst_ref=other, send_sem=send_sem, recv_sem=recv_sem,
        device_id={"head": 1 - head}, device_id_type=pl.DeviceIdType.MESH)
    swap.start()
    weights.wait()
    mine = pl.ds(pl.multiple_of(head * width, width), width)
    theirs = pl.ds(pl.multiple_of((1 - head) * width, width), width)
    total[...] = jnp.dot(att_ref[...], w_buf[mine, :], preferred_element_type=jnp.float32)
    swap.wait()
    out_ref[...] = (
        total[...] + jnp.dot(other[...], w_buf[theirs, :], preferred_element_type=jnp.float32)).astype(jnp.bfloat16)


def body(query_input, key_input, value_input, cube_lists, coarse_gate, out_weight):
    lists = jnp.transpose(cube_lists, (1, 0, 2)).reshape(HEADS, CUBES * TOP)
    any_spec = pl.BlockSpec(memory_space=pl.ANY)
    vmem_spec = pl.BlockSpec(memory_space=pltpu.VMEM)
    smem_spec = pl.BlockSpec(memory_space=pltpu.SMEM)
    dma = pltpu.SemaphoreType.DMA
    recv, coarse, count, slots, cubes, part, stat = pl.pallas_call(
        exchange,
        out_shape=(
            jax.ShapeDtypeStruct((2, PLANE * len(LATE) * SLOTS, TOK, HD), jnp.bfloat16),
            jax.ShapeDtypeStruct((UNITS, HD), jnp.float32),
            jax.ShapeDtypeStruct((HEADS, 128), jnp.int32),
            jax.ShapeDtypeStruct((HEADS, 256), jnp.int32),
            jax.ShapeDtypeStruct((HEADS, 256), jnp.int32),
            jax.ShapeDtypeStruct((UNITS, TOK, HD), jnp.float32),
            jax.ShapeDtypeStruct((UNITS, TOK, HD), jnp.float32),
        ),
        in_specs=[any_spec] * 3 + [vmem_spec],
        out_specs=(any_spec,) + (vmem_spec,) * 6,
        scratch_shapes=[pltpu.VMEM((UNITS, TOK, HD), jnp.bfloat16)] * 17 + [
            pltpu.VMEM((2, NZ, PLANE, SLOTS, TOK, HD), jnp.bfloat16),
            pltpu.VMEM((2, len(EARLY) * PLANE * SLOTS, TOK, HD), jnp.bfloat16),
            pltpu.VMEM((8, 128), jnp.int32),
            pltpu.VMEM((UNITS, 128), jnp.float32),
            pltpu.VMEM((UNITS, 128), jnp.float32),
            pltpu.VMEM((8, 256), jnp.int32),
            pltpu.SMEM((8, 256), jnp.int32),
            pltpu.VMEM((PLANE, 8, 128), jnp.int32),
            pltpu.SMEM((PLANE, 8, 128), jnp.int32),
            pltpu.VMEM((PLANE, UNITS, HD), jnp.float32),
            pltpu.VMEM((HEADS, NZ * CUBES, HD), jnp.float32),
            pltpu.VMEM((HEADS, NZ * CUBES, HD), jnp.float32),
            pltpu.VMEM((PLANE, UNITS, HD), jnp.float32),
            pltpu.VMEM((PLANE, UNITS, HD), jnp.bfloat16),
            pltpu.VMEM((PLANE, UNITS, HD), jnp.bfloat16),
            pltpu.VMEM((PLANE, CUBES, HD), jnp.float32),
            pltpu.VMEM((PLANE, CUBES, HD), jnp.float32),
            dma((18,)), dma((28,)), dma((28,)), dma((PLANE,)), dma((PLANE,)), dma((PLANE,)), dma((PLANE,)),
            dma((2, NZ, PLANE)), dma((2, NZ, PLANE)), dma((PLANE,)), dma((PLANE,)), dma((PLANE,)), dma((PLANE,)), dma, dma, dma((2, len(LATE))),
        ],
        compiler_params=pltpu.CompilerParams(
            collective_id=0, has_side_effects=True, vmem_limit_bytes=56 * 1024 * 1024),
        name="exchange",
    )(*[t.reshape(CUBES, TOK, HEADS * HD) for t in (query_input, key_input, value_input)], lists)
    attended = pl.pallas_call(
        fine,
        out_shape=jax.ShapeDtypeStruct((CUBES * TOK, HEADS * HD), jnp.bfloat16),
        in_specs=[smem_spec] * 4 + [vmem_spec] * 4 + [any_spec],
        out_specs=vmem_spec,
        scratch_shapes=[
            pltpu.VMEM((2, PLANE * len(LATE) * SLOTS, TOK, HD), jnp.bfloat16),
            pltpu.VMEM((RING, GROUP // 2, CUBES * TOK, HD), jnp.float32),
        ] + [pltpu.VMEM((HEADS, CUBES * TOK, HD), jnp.float32)] + [pltpu.VMEM((CUBES * TOK, HD), jnp.float32)] * 3
        + [dma((2,))],
        compiler_params=pltpu.CompilerParams(vmem_limit_bytes=56 * 1024 * 1024),
        name="fine",
    )(count, slots, cubes, coarse_gate, query_input, part, stat, coarse, recv)
    shape = (CUBES * TOK, HEADS * HD)
    return pl.pallas_call(
        project,
        out_shape=jax.ShapeDtypeStruct(shape, jnp.bfloat16),
        in_specs=[vmem_spec, any_spec],
        out_specs=vmem_spec,
        scratch_shapes=[
            pltpu.VMEM(shape, jnp.bfloat16),
            pltpu.VMEM((2 * HEADS * HD, HEADS * HD), jnp.bfloat16),
            pltpu.VMEM(shape, jnp.float32),
            dma, dma, dma,
        ],
        compiler_params=pltpu.CompilerParams(
            collective_id=1, has_side_effects=True, vmem_limit_bytes=48 * 1024 * 1024),
        name="project",
    )(attended, out_weight)


def solution(mesh):
    placed = (
        P("seq", "head"),
        P("seq", "head"),
        P("seq", "head"),
        P("seq", "head", None),
        P("head"),
        P(),
    )
    return jax.shard_map(
        body, mesh=mesh, in_specs=placed, out_specs=P("seq", "head"), check_vma=False
    )
```

```python
import functools

import jax
import jax.numpy as jnp
from jax import lax
from jax.experimental import pallas as pl
from jax.experimental.pallas import tpu as pltpu
from jax.sharding import PartitionSpec as P

NX, NY, NZ = 4, 4, 8
PLANE = NX * NY
SLOTS = 3
CUBES = 8
HEADS = 6
TOK = 64
HD = 128
TOP = 32
UNITS = CUBES * HEADS
MAXU = 144
GROUP = 8
RING = MAXU // GROUP
NEG = -1e30
AHEAD = 4
EARLY = {0: 0, 1: 1, 2: 2, 4: 3, 5: 4}
LATE = {3: 0, 6: 1, 7: 2}
SAFE = PLANE * SLOTS
SCALE = HD ** -0.5
LOG2E = 1.4426950408889634
NT = (((1,), (1,)), ((), ()))


def iota(shape, dim):
    return lax.broadcasted_iota(jnp.int32, shape, dim)


def flag(mask):
    return jnp.where(mask, 1.0, 0.0).astype(jnp.bfloat16)


def list_rows(lists_ref, owner_ref, within_ref):
    spread = flag((iota((TOP, 256), 1) & (TOP - 1)) == iota((TOP, 256), 0))
    mine = (iota((CUBES, 256), 1) >> 5) == iota((CUBES, 256), 0)
    for h in range(HEADS):
        cubes = lists_ref[:, h, :]
        for part, ref in ((cubes >> 3, owner_ref), (cubes & 7, within_ref)):
            wide = jnp.dot(part.astype(jnp.float32).astype(jnp.bfloat16), spread, preferred_element_type=jnp.float32)
            ref[h:h + 1, :] = jnp.sum(jnp.where(mine, wide, 0.0), axis=0, keepdims=True).astype(jnp.int32)


def unit_slots(z, owner_ref, within_ref, table_ref, bits_ref, rank_ref, pos_ref):
    entry_bit = 1 << (iota((CUBES, 256), 1) >> 5)
    bits, hots = [], []
    for h in range(HEADS):
        owner_hot = flag(owner_ref[h:h + 1, :] == iota((128, 256), 0))
        hots.append(owner_hot)
        within_bit = jnp.where(within_ref[h:h + 1, :] == iota((CUBES, 256), 0), entry_bit, 0)
        bits.append(lax.dot_general(within_bit.astype(jnp.float32).astype(jnp.bfloat16), owner_hot, NT,
                                    preferred_element_type=jnp.float32))
    bits = jnp.concatenate(bits, axis=0)
    need = bits > 0
    lower = flag(iota((UNITS, UNITS), 0) >= iota((UNITS, UNITS), 1))
    rank = jnp.dot(lower, flag(need), preferred_element_type=jnp.float32)
    bits_ref[...] = bits
    rank_ref[...] = rank
    unit = iota((UNITS, 128), 0)
    table_ref[...] = jnp.zeros_like(table_ref)
    for s in range(SLOTS):
        table_ref[s:s + 1, :] = jnp.sum(jnp.where(need & (rank == s + 1), unit, 0), axis=0, keepdims=True)
    pos_ref[...] = jnp.zeros_like(pos_ref)
    for h in range(HEADS):
        owner = owner_ref[h:h + 1, :]
        spread = jnp.dot(rank[h * 8:h * 8 + 8].astype(jnp.bfloat16), hots[h], preferred_element_type=jnp.float32)
        here = jnp.where(within_ref[h:h + 1, :] == iota((CUBES, 256), 0), spread, 0.0)
        order = jnp.sum(here, axis=0, keepdims=True).astype(jnp.int32) - 1
        ahead = (((owner >> 2) & 7) - z) & 7
        which = jnp.where(ahead == 0, 0, jnp.where(ahead >= 6, 8 - ahead, ahead + 2))
        column = (owner >> 5) * NX + (owner & 3)
        late = (ahead >= 3) & (ahead <= 5)
        pos_ref[h:h + 1, :] = jnp.where(late, -1, (which * PLANE + column) * SLOTS + order)


def head_lists(z, bits_ref, rank_ref, count_ref, slots_ref, cubes_ref):
    bits, rank = bits_ref[...], rank_ref[...]
    need = bits > 0
    ahead = (((iota((UNITS, 128), 1) >> 2) & 7) - z) & 7
    late = (ahead >= 3) & (ahead <= 5)
    mine, mine_bits = [], []
    for s in range(SLOTS):
        hit = jnp.where(need & (rank == s + 1) & late, 1.0, 0.0)
        seen = hit * bits
        mine.append([jnp.sum(hit[h * 8:h * 8 + 8], axis=0, keepdims=True) for h in range(HEADS)])
        mine_bits.append([jnp.sum(seen[h * 8:h * 8 + 8], axis=0, keepdims=True) for h in range(HEADS)])
    wide = SLOTS * 128
    upper = flag(iota((wide, wide), 0) <= iota((wide, wide), 1))
    lane = iota((1, wide), 1)
    owner = lane & 127
    ahead = (((owner >> 2) & 7) - z) & 7
    index = jnp.where(ahead == 5, 0, jnp.where(ahead == 3, 1, 2))
    place = ((owner >> 5) * NX + (owner & 3)) * len(LATE) + index
    place = jnp.broadcast_to(place.astype(jnp.float32), (8, wide))
    slot = jnp.broadcast_to((lane >> 7).astype(jnp.float32), (8, wide))
    sub = iota((8, wide), 0)
    for h in range(HEADS):
        have = jnp.concatenate([mine[s][h] for s in range(SLOTS)], axis=1)
        have_bits = jnp.concatenate([mine_bits[s][h] for s in range(SLOTS)], axis=1)
        have8 = jnp.broadcast_to(have, (8, wide))
        order = jnp.dot(have8.astype(jnp.bfloat16), upper, preferred_element_type=jnp.float32)
        want = (iota((256, wide), 0) + 1).astype(jnp.float32)
        hit = jnp.where((order[0:1, :] == want) & (have > 0), 1.0, 0.0).astype(jnp.bfloat16)
        facts = jnp.where(sub == 0, place, jnp.where(sub == 1, slot, jnp.broadcast_to(have_bits, (8, wide))))
        facts = lax.dot_general(facts.astype(jnp.bfloat16), hit, NT, preferred_element_type=jnp.float32)
        slots_ref[h:h + 1, :] = (facts[0:1, :] * SLOTS + facts[1:2, :]).astype(jnp.int32)
        cubes_ref[h:h + 1, :] = facts[2:3, :].astype(jnp.int32)
        total = jnp.sum(have, axis=1, keepdims=True)
        count_ref[h:h + 1, :] = jnp.broadcast_to(total, (1, 128)).astype(jnp.int32)


def exchange(
    q_hbm, k_hbm, v_hbm, lists_ref, recv, coarse_ref, count_ref, slots_ref, cubes_ref, part_ref, stat_ref, *scratch
):
    q_own = scratch[0]
    kk = scratch[1:9]
    vv = scratch[9:17]
    (send_buf, early, owner_rows, within_rows, tbl_ref, bits_ref, rank_ref, pos_ref, pos_sm, tbl_all, tbl_sm, q_all, pool_k, pool_v, o_res, o_half, o_got, stats, stats_all,
     load_sem, z_send, z_recv, t_send, t_recv, q_send, q_recv, u_send, u_recv,
     o_send, o_recv, m_send, m_recv, sm_sem, pos_sem, loc_sem) = scratch[17:]
    s = lax.axis_index("seq")
    x = lax.rem(s, NX)
    z = lax.rem(lax.div(s, NX), NZ)
    y = lax.div(s, NX * NZ)
    me = y * NX + x

    def peer(j):
        px = lax.rem(x + lax.rem(j, NX), NX)
        py = lax.rem(y + lax.div(j, NX), NY)
        return py * NX + px, (py * NZ + z) * NX + px

    def remote(src, dst, send, recv_, seq):
        return pltpu.make_async_remote_copy(
            src_ref=src, dst_ref=dst, send_sem=send, recv_sem=recv_,
            device_id={"seq": seq}, device_id_type=pl.DeviceIdType.MESH,
        )

    right = (y * NZ + lax.rem(z + 1, NZ)) * NX + x
    left = (y * NZ + lax.rem(z + NZ - 1, NZ)) * NX + x

    loads = []
    for i, (src, dst) in enumerate(((k_hbm, kk[0]), (v_hbm, vv[0]), (q_hbm, q_own))):
        for h in range(HEADS):
            loads.append(pltpu.make_async_copy(
                src.at[:, :, pl.ds(h * HD, HD)], dst.at[pl.ds(h * CUBES, CUBES)], load_sem.at[i * HEADS + h]))
    for c in loads:
        c.start()

    barrier = pltpu.get_barrier_semaphore()
    for seq in (right, left):
        pl.semaphore_signal(barrier, inc=1, device_id={"seq": seq}, device_id_type=pl.DeviceIdType.MESH)

    @pl.loop(1, PLANE)
    def _(j):
        pl.semaphore_signal(barrier, inc=1, device_id={"seq": peer(j)[1]}, device_id_type=pl.DeviceIdType.MESH)

    list_rows(lists_ref, owner_rows, within_rows)
    unit_slots(z, owner_rows, within_rows, tbl_ref, bits_ref, rank_ref, pos_ref)
    pl.semaphore_wait(barrier, PLANE + 1)

    @pl.loop(1, PLANE)
    def _(j):
        pp, seq = peer(j)
        remote(tbl_ref, tbl_all.at[me], t_send.at[j], t_recv.at[me], seq).start()

    def ring(first, second, base, far, seq, sem0):
        out = []
        for n in range(14):
            vals = first if n % 4 < 2 else second
            stage = n // 4
            src = vals[0 if stage == 0 else base + stage - 1]
            dst = vals[base + stage if stage < 3 else far]
            part = pl.ds((n % 2) * 24, 24)
            out.append(remote(src.at[part], dst.at[part], z_send.at[sem0 + n], z_recv.at[sem0 + n], seq))
        return out

    to_right = ring(kk, vv, 1, 7, right, 0)
    to_left = ring(vv, kk, 4, 7, left, 14)

    for c in loads[:2 * HEADS]:
        c.wait()
    for n in range(AHEAD):
        to_right[n].start()
        to_left[n].start()

    tbl_all[me] = tbl_ref[...]
    for c in loads[2 * HEADS:]:
        c.wait()

    row = lax.broadcasted_iota(jnp.int32, (CUBES, 512), 0)
    col = lax.broadcasted_iota(jnp.int32, (CUBES, 512), 1)
    mean = jnp.where(lax.div(col, TOK) == row, 1.0 / TOK, 0.0).astype(jnp.bfloat16)

    @pl.loop(0, HEADS)
    def _(h):
        q_all[me, pl.ds(h * CUBES, CUBES), :] = jnp.dot(
            mean, q_own[pl.ds(h * CUBES, CUBES)].reshape(512, HD), preferred_element_type=jnp.float32)

    @pl.loop(1, PLANE)
    def _(j):
        pp, seq = peer(j)
        remote(q_all.at[me], q_all.at[me], q_send.at[j], q_recv.at[me], seq).start()

    @pl.loop(1, PLANE)
    def _(j):
        pp, seq = peer(j)
        remote(tbl_ref, tbl_all.at[pp], t_send.at[j], t_recv.at[pp], seq).wait()

    to_smem_pos = pltpu.make_async_copy(pos_ref, pos_sm, pos_sem)
    to_smem_pos.start()
    to_smem = pltpu.make_async_copy(tbl_all, tbl_sm, sm_sem)
    to_smem.start()
    to_smem.wait()
    to_smem_pos.wait()

    def owner_z(k):
        if k <= 3:
            return lax.rem(z + NZ - k, NZ)
        if k <= 6:
            return lax.rem(z + k - 3, NZ)
        return lax.rem(z + 4, NZ)

    def unit_of(k, val, pp, sl):
        lane = (y * NZ + owner_z(k)) * NX + x
        return (vv[k] if val else kk[k])[jnp.clip(tbl_sm[pp, sl, lane], 0, UNITS - 1)]

    def landing(k, val, p):
        if k in EARLY:
            return early.at[val, pl.ds((EARLY[k] * PLANE + p) * SLOTS, SLOTS)]
        return recv.at[val, pl.ds((p * len(LATE) + LATE[k]) * SLOTS, SLOTS)]

    def own_copy(k, val):
        return pltpu.make_async_copy(send_buf.at[val, k, me], landing(k, val, me), loc_sem.at[val, LATE[k]])

    def handle(k, val):
        @pl.loop(1, PLANE)
        def _(j):
            pp, seq = peer(j)
            for sl in range(SLOTS):
                send_buf[val, k, pp, sl] = unit_of(k, val, pp, sl)
            remote(send_buf.at[val, k, pp], landing(k, val, me), u_send.at[val, k, j], u_recv.at[val, k, me], seq).start()

        for sl in range(SLOTS):
            if k in LATE:
                send_buf[val, k, me, sl] = unit_of(k, val, me, sl)
            elif k > 0:
                early[val, (EARLY[k] * PLANE + me) * SLOTS + sl] = unit_of(k, val, me, sl)
        if k in LATE:
            own_copy(k, val).start()

    def arrived(k, val):
        @pl.loop(1, PLANE)
        def _(j):
            pp, seq = peer(j)
            remote(send_buf.at[val, k, pp], landing(k, val, pp), u_send.at[val, k, j], u_recv.at[val, k, pp], seq).wait_recv()

    low_lanes = iota((1, 128), 1) < TOK

    def attend(i):
        h, c = lax.div(i, CUBES), lax.rem(i, CUBES)
        q = q_own[i]
        scores = [lax.dot_general(q, kk[0][i], NT, preferred_element_type=jnp.float32)]
        spots = [pos_sm[h, c * TOP + t] for t in range(TOP)]
        where = [jnp.clip(jnp.where(p < 0, SAFE, p), 0, len(EARLY) * PLANE * SLOTS - 1) for p in spots]
        bias = [jnp.where(p < 0, NEG, 0.0) for p in spots]
        for g in range(TOP // 4):
            keys = jnp.concatenate([early[0, where[4 * g + t]] for t in range(4)], axis=0)
            sc = lax.dot_general(q, keys, NT, preferred_element_type=jnp.float32)
            hide = jnp.concatenate(
                [jnp.where(low_lanes, bias[4 * g + t], bias[4 * g + t + 1]) for t in (0, 2)], axis=1)
            scores.append(sc + hide)
        top = functools.reduce(jnp.maximum, scores[1:])
        top = jnp.maximum(jnp.max(top, axis=1, keepdims=True), jnp.max(scores[0], axis=1, keepdims=True))
        es = [jnp.exp2((sc - top) * (SCALE * LOG2E)) for sc in scores]
        tot = jnp.sum(es[0], axis=1, keepdims=True) + jnp.sum(sum(es[2:], es[1]), axis=1, keepdims=True)
        acc = jnp.dot(es[0].astype(jnp.bfloat16), vv[0][i], preferred_element_type=jnp.float32)
        for g in range(TOP // 4):
            vals = jnp.concatenate([early[1, where[4 * g + t]] for t in range(4)], axis=0)
            acc += jnp.dot(es[g + 1].astype(jnp.bfloat16), vals, preferred_element_type=jnp.float32)
        part_ref[i] = acc
        stat_ref[i] = jnp.where(low_lanes, top, tot)

    def attend_range(lo, hi):
        @pl.loop(lo, hi)
        def _(i):
            attend(i)

    def pool(k, val):
        src, dst = (vv[k], pool_v) if val else (kk[k], pool_k)

        @pl.loop(0, HEADS)
        def _(h):
            dst[h, pl.ds(k * CUBES, CUBES), :] = jnp.dot(
                mean, src[pl.ds(h * CUBES, CUBES)].reshape(512, HD), preferred_element_type=jnp.float32)

    handle(0, 0)
    handle(0, 1)
    pool(0, 0)
    pool(0, 1)
    head_lists(z, bits_ref, rank_ref, count_ref, slots_ref, cubes_ref)
    for n in range(14):
        for way in (to_right, to_left):
            way[n].wait_recv()
            if n + AHEAD < 14:
                way[n + AHEAD].start()
        if n % 2:
            stage = n // 4
            val = (n % 4) // 2
            for k, which in ((1 + stage if stage < 3 else 7, val), (4 + stage if stage < 3 else 7, 1 - val)):
                if stage < 3:
                    handle(k, which)
                pool(k, which)
        if n == 10:
            for k in EARLY:
                arrived(k, 0)
                arrived(k, 1)
            attend_range(0, 8)
        if n == 11:
            attend_range(8, 22)
        if n == 12:
            attend_range(22, 30)

    @pl.loop(1, PLANE)
    def _(j):
        pp, seq = peer(j)
        remote(q_all.at[me], q_all.at[pp], q_send.at[j], q_recv.at[pp], seq).wait()

    lane3 = lax.broadcasted_iota(jnp.int32, (PLANE * CUBES, HD), 1)

    def coarse_head(h, stat):
        rows = pl.ds(pl.multiple_of(h * CUBES, CUBES), CUBES)
        qh = q_all[:, rows, :].reshape(PLANE * CUBES, HD)
        sc = lax.dot_general(qh, pool_k[h], NT, precision=lax.Precision.HIGHEST,
                             preferred_element_type=jnp.float32) * SCALE
        top = jnp.max(sc, axis=1, keepdims=True)
        e = jnp.exp(sc - top)
        tot = jnp.sum(e, axis=1, keepdims=True)
        o = jnp.dot(e, pool_v[h], precision=lax.Precision.HIGHEST, preferred_element_type=jnp.float32)
        o_res[:, rows, :] = o.reshape(PLANE, CUBES, HD)
        stat = jnp.where(lane3 == h, top, stat)
        return jnp.where(lane3 == h + 64, tot, stat)

    stat = lax.fori_loop(0, HEADS, coarse_head, jnp.zeros((PLANE * CUBES, HD), jnp.float32))
    stats[...] = stat.reshape(PLANE, CUBES, HD)
    o_half[...] = o_res[...].astype(jnp.bfloat16)

    @pl.loop(1, PLANE)
    def _(j):
        pp, seq = peer(j)
        remote(o_half.at[pp], o_got.at[me], o_send.at[j], o_recv.at[me], seq).start()
        remote(stats.at[pp], stats_all.at[me], m_send.at[j], m_recv.at[me], seq).start()

    handle(7, 0)
    handle(7, 1)
    attend_range(30, UNITS)
    o_got[me] = o_half[me]
    stats_all[me] = stats[me]

    @pl.loop(1, PLANE)
    def _(j):
        pp, seq = peer(j)
        remote(o_half.at[pp], o_got.at[pp], o_send.at[j], o_recv.at[pp], seq).wait()
        remote(stats.at[pp], stats_all.at[pp], m_send.at[j], m_recv.at[pp], seq).wait()

    o_res[...] = o_got[...].astype(jnp.float32)
    for h in range(HEADS):
        top = stats_all[:, :, h:h + 1]
        tot = stats_all[:, :, 64 + h:65 + h]
        w = jnp.exp(top - jnp.max(top, axis=0, keepdims=True))
        den = jnp.sum(w * tot, axis=0)
        num = jnp.sum(w * o_res[:, pl.ds(h * CUBES, CUBES), :], axis=0)
        coarse_ref[pl.ds(h * CUBES, CUBES), :] = num / den

    for c in to_right + to_left:
        c.wait_send()
    for k in range(NZ):
        for val in range(2):
            if k in LATE:
                own_copy(k, val).wait()
                arrived(k, val)

            @pl.loop(1, PLANE)
            def _(j):
                pp, seq = peer(j)
                remote(send_buf.at[val, k, pp], landing(k, val, me), u_send.at[val, k, j], u_recv.at[val, k, me], seq).wait_send()


def fine(count_ref, slot_ref, bits_ref, gate_ref, q_ref, stat_ref, coarse_ref, part_hbm, recv_hbm, out_ref,
         recv, part_ref, s_buf, top, peak, tot, acc, sem):
    c2 = SCALE * LOG2E
    pairs = GROUP // 2
    copies = [pltpu.make_async_copy(recv_hbm.at[i], recv.at[i], sem.at[i]) for i in range(2)]
    copies.append(pltpu.make_async_copy(part_hbm, part_ref, sem.at[2]))
    for c in copies:
        c.start()
    lane = lax.broadcasted_iota(jnp.int32, (1, 128), 1)

    def columns(h):
        return pl.ds(pl.multiple_of(h * HD, HD), HD)

    def blocks(h):
        return jnp.maximum(lax.div(count_ref[jnp.minimum(h, HEADS - 1), 0] + GROUP - 1, GROUP), 1)

    def step(at):
        h, g = at
        last = g + 1 >= blocks(h)
        return jnp.where(last, h + 1, h), jnp.where(last, 0, g + 1)

    def units(val, h, g):
        return jnp.concatenate(
            [recv[val, slot_ref[h, jnp.clip(count_ref[h, 0] - 1, 0, g * GROUP + t)]] for t in range(GROUP)], axis=0)

    def score(i, at):
        h, g = at
        slot = lax.rem(i, RING)
        sc = lax.dot_general(q_ref[:, columns(h)], units(0, h, g), NT, preferred_element_type=jnp.float32)
        rowbits = [
            jnp.where(lane < TOK, bits_ref[h, g * GROUP + 2 * t], bits_ref[h, g * GROUP + 2 * t + 1])
            for t in range(pairs)
        ]
        for c in range(CUBES):
            rows = pl.ds(c * TOK, TOK)
            best = top[h, rows, :]
            for t in range(pairs):
                bias = jnp.where((rowbits[t] >> c) & 1 == 1, 0.0, NEG)
                part = sc[c * TOK:(c + 1) * TOK, t * 128:(t + 1) * 128] + bias
                s_buf[slot, t, rows, :] = part
                best = jnp.maximum(best, part)
            top[h, rows, :] = best

    def begin(at):
        h, g = at

        @pl.when(g == 0)
        def _():
            peak[...] = jnp.broadcast_to(jnp.max(top[h], axis=1, keepdims=True) * c2, (CUBES * TOK, HD))
            for c in range(CUBES):
                rows = pl.ds(c * TOK, TOK)
                state = stat_ref[h * CUBES + c]
                shrink = jnp.exp2(state[:, 0:1] * c2 - peak[rows, :])
                tot[rows, :] = shrink * jnp.where(lane < TOK, 0.0, state * (1.0 / TOK))
                acc[rows, :] = shrink * part_ref[h * CUBES + c]

    def value(i, at):
        h, g = at
        slot = lax.rem(i, RING)
        blocks_of_rows = []
        for c in range(CUBES):
            rows = pl.ds(c * TOK, TOK)
            high, sums, parts = peak[rows, :], tot[rows, :], []
            for t in range(pairs):
                e = jnp.exp2(s_buf[slot, t, rows, :] * c2 - high)
                sums += e
                parts.append(e.astype(jnp.bfloat16))
            tot[rows, :] = sums
            blocks_of_rows.append(jnp.concatenate(parts, axis=1))
        acc[...] += jnp.dot(
            jnp.concatenate(blocks_of_rows, axis=0), units(1, h, g), preferred_element_type=jnp.float32)

    def finish(at):
        h, g = at

        @pl.when(g + 1 == blocks(h))
        def _():
            for c in range(CUBES):
                rows = pl.ds(c * TOK, TOK)
                total = jnp.sum(tot[rows, :], axis=1, keepdims=True)
                pooled = gate_ref[h] * coarse_ref[pl.ds(h * CUBES + c, 1), :]
                out_ref[rows, columns(h)] = (acc[rows, :] / total + pooled).astype(jnp.bfloat16)

    @pl.loop(0, UNITS)
    def _(i):
        rows = pl.ds(pl.multiple_of(lax.rem(i, CUBES) * TOK, TOK), TOK)
        top[lax.div(i, CUBES), rows, :] = jnp.where(lane < TOK, stat_ref[i], NEG)

    longest, items = blocks(0), blocks(0)
    for h in range(1, HEADS):
        longest, items = jnp.maximum(longest, blocks(h)), items + blocks(h)
    copies[0].wait()

    def only_score(i, at):
        score(i, at)
        return step(at)

    def both(i, carry):
        ahead, at = carry
        begin(at)
        value(i - longest, at)
        score(i, ahead)
        finish(at)
        return step(ahead), step(at)

    def only_value(i, at):
        begin(at)
        value(i - longest, at)
        finish(at)
        return step(at)

    zero = jnp.int32(0)
    ahead = lax.fori_loop(0, longest, only_score, (zero, zero))
    copies[1].wait()
    copies[2].wait()
    ahead, at = lax.fori_loop(longest, items, both, (ahead, (zero, zero)))
    lax.fori_loop(items, items + longest, only_value, at)


def project(att_hbm, w_hbm, out_ref, own, other, w_buf, total, send_sem, recv_sem, w_sem, own_sem):
    head = lax.axis_index("head")
    width = HEADS * HD
    weights = pltpu.make_async_copy(w_hbm.at[:, pl.ds(pl.multiple_of(head * width, width), width)], w_buf, w_sem)
    fetch = pltpu.make_async_copy(att_hbm, own, own_sem)
    fetch.start()
    weights.start()
    barrier = pltpu.get_barrier_semaphore()
    pl.semaphore_signal(barrier, inc=1, device_id={"head": 1 - head}, device_id_type=pl.DeviceIdType.MESH)
    pl.semaphore_wait(barrier, 1)
    swap = pltpu.make_async_remote_copy(
        src_ref=att_hbm, dst_ref=other, send_sem=send_sem, recv_sem=recv_sem,
        device_id={"head": 1 - head}, device_id_type=pl.DeviceIdType.MESH)
    swap.start()
    fetch.wait()
    weights.wait()
    mine = pl.ds(pl.multiple_of(head * width, width), width)
    theirs = pl.ds(pl.multiple_of((1 - head) * width, width), width)
    total[...] = jnp.dot(own[...], w_buf[mine, :], preferred_element_type=jnp.float32)
    swap.wait()
    out_ref[...] = (
        total[...] + jnp.dot(other[...], w_buf[theirs, :], preferred_element_type=jnp.float32)).astype(jnp.bfloat16)


def body(query_input, key_input, value_input, cube_lists, coarse_gate, out_weight):
    any_spec = pl.BlockSpec(memory_space=pl.ANY)
    vmem_spec = pl.BlockSpec(memory_space=pltpu.VMEM)
    smem_spec = pl.BlockSpec(memory_space=pltpu.SMEM)
    dma = pltpu.SemaphoreType.DMA
    recv, coarse, count, slots, cubes, part, stat = pl.pallas_call(
        exchange,
        out_shape=(
            jax.ShapeDtypeStruct((2, PLANE * len(LATE) * SLOTS, TOK, HD), jnp.bfloat16),
            jax.ShapeDtypeStruct((UNITS, HD), jnp.float32),
            jax.ShapeDtypeStruct((HEADS, 128), jnp.int32),
            jax.ShapeDtypeStruct((HEADS, 256), jnp.int32),
            jax.ShapeDtypeStruct((HEADS, 256), jnp.int32),
            jax.ShapeDtypeStruct((UNITS, TOK, HD), jnp.float32),
            jax.ShapeDtypeStruct((UNITS, TOK, HD), jnp.float32),
        ),
        in_specs=[any_spec] * 3 + [vmem_spec],
        out_specs=(any_spec,) + (vmem_spec,) * 6,
        scratch_shapes=[pltpu.VMEM((UNITS, TOK, HD), jnp.bfloat16)] * 17 + [
            pltpu.VMEM((2, NZ, PLANE, SLOTS, TOK, HD), jnp.bfloat16),
            pltpu.VMEM((2, len(EARLY) * PLANE * SLOTS, TOK, HD), jnp.bfloat16),
            pltpu.VMEM((8, 256), jnp.int32),
            pltpu.VMEM((8, 256), jnp.int32),
            pltpu.VMEM((8, 128), jnp.int32),
            pltpu.VMEM((UNITS, 128), jnp.float32),
            pltpu.VMEM((UNITS, 128), jnp.float32),
            pltpu.VMEM((8, 256), jnp.int32),
            pltpu.SMEM((8, 256), jnp.int32),
            pltpu.VMEM((PLANE, 8, 128), jnp.int32),
            pltpu.SMEM((PLANE, 8, 128), jnp.int32),
            pltpu.VMEM((PLANE, UNITS, HD), jnp.float32),
            pltpu.VMEM((HEADS, NZ * CUBES, HD), jnp.float32),
            pltpu.VMEM((HEADS, NZ * CUBES, HD), jnp.float32),
            pltpu.VMEM((PLANE, UNITS, HD), jnp.float32),
            pltpu.VMEM((PLANE, UNITS, HD), jnp.bfloat16),
            pltpu.VMEM((PLANE, UNITS, HD), jnp.bfloat16),
            pltpu.VMEM((PLANE, CUBES, HD), jnp.float32),
            pltpu.VMEM((PLANE, CUBES, HD), jnp.float32),
            dma((18,)), dma((28,)), dma((28,)), dma((PLANE,)), dma((PLANE,)), dma((PLANE,)), dma((PLANE,)),
            dma((2, NZ, PLANE)), dma((2, NZ, PLANE)), dma((PLANE,)), dma((PLANE,)), dma((PLANE,)), dma((PLANE,)), dma, dma, dma((2, len(LATE))),
        ],
        compiler_params=pltpu.CompilerParams(
            collective_id=0, has_side_effects=True, vmem_limit_bytes=56 * 1024 * 1024),
        name="exchange",
    )(*[t.reshape(CUBES, TOK, HEADS * HD) for t in (query_input, key_input, value_input)], cube_lists)
    attended = pl.pallas_call(
        fine,
        out_shape=jax.ShapeDtypeStruct((CUBES * TOK, HEADS * HD), jnp.bfloat16),
        in_specs=[smem_spec] * 4 + [vmem_spec] * 3 + [any_spec] * 2,
        out_specs=vmem_spec,
        scratch_shapes=[
            pltpu.VMEM((2, PLANE * len(LATE) * SLOTS, TOK, HD), jnp.bfloat16),
            pltpu.VMEM((UNITS, TOK, HD), jnp.float32),
            pltpu.VMEM((RING, GROUP // 2, CUBES * TOK, HD), jnp.float32),
        ] + [pltpu.VMEM((HEADS, CUBES * TOK, HD), jnp.float32)] + [pltpu.VMEM((CUBES * TOK, HD), jnp.float32)] * 3
        + [dma((3,))],
        compiler_params=pltpu.CompilerParams(vmem_limit_bytes=56 * 1024 * 1024),
        name="fine",
    )(count, slots, cubes, coarse_gate, query_input, stat, coarse, part, recv)
    shape = (CUBES * TOK, HEADS * HD)
    return pl.pallas_call(
        project,
        out_shape=jax.ShapeDtypeStruct(shape, jnp.bfloat16),
        in_specs=[pl.BlockSpec(memory_space=pltpu.HBM)] * 2,
        out_specs=vmem_spec,
        scratch_shapes=[
            pltpu.VMEM(shape, jnp.bfloat16),
            pltpu.VMEM(shape, jnp.bfloat16),
            pltpu.VMEM((2 * HEADS * HD, HEADS * HD), jnp.bfloat16),
            pltpu.VMEM(shape, jnp.float32),
            dma, dma, dma, dma,
        ],
        compiler_params=pltpu.CompilerParams(
            collective_id=1, has_side_effects=True, vmem_limit_bytes=48 * 1024 * 1024),
        name="project",
    )(attended, out_weight)


def solution(mesh):
    placed = (
        P("seq", "head"),
        P("seq", "head"),
        P("seq", "head"),
        P("seq", "head", None),
        P("head"),
        P(),
    )
    return jax.shard_map(
        body, mesh=mesh, in_specs=placed, out_specs=P("seq", "head"), check_vma=False
    )
```

```python
import functools

import jax
import jax.numpy as jnp
from jax import lax
from jax.experimental import pallas as pl
from jax.experimental.pallas import tpu as pltpu
from jax.sharding import PartitionSpec as P

NX, NY, NZ = 4, 4, 8
PLANE = NX * NY
SLOTS = 3
CUBES = 8
HEADS = 6
TOK = 64
HD = 128
TOP = 32
UNITS = CUBES * HEADS
MAXU = 144
GROUP = 8
RING = MAXU // GROUP
NEG = -1e30
AHEAD = 4
EARLY = {0: 0, 1: 1, 2: 2, 4: 3, 5: 4}
LATE = {3: 0, 6: 1, 7: 2}
SAFE = PLANE * SLOTS
SCALE = HD ** -0.5
LOG2E = 1.4426950408889634
NT = (((1,), (1,)), ((), ()))


def iota(shape, dim):
    return lax.broadcasted_iota(jnp.int32, shape, dim)


def flag(mask):
    return jnp.where(mask, 1.0, 0.0).astype(jnp.bfloat16)


def list_rows(lists_ref, owner_ref, within_ref):
    spread = flag((iota((TOP, 256), 1) & (TOP - 1)) == iota((TOP, 256), 0))
    mine = (iota((CUBES, 256), 1) >> 5) == iota((CUBES, 256), 0)
    for h in range(HEADS):
        cubes = lists_ref[h]
        for part, ref in ((cubes >> 3, owner_ref), (cubes & 7, within_ref)):
            wide = jnp.dot(part.astype(jnp.float32).astype(jnp.bfloat16), spread, preferred_element_type=jnp.float32)
            ref[h:h + 1, :] = jnp.sum(jnp.where(mine, wide, 0.0), axis=0, keepdims=True).astype(jnp.int32)


def unit_slots(z, owner_ref, within_ref, table_ref, bits_ref, rank_ref, pos_ref):
    entry_bit = 1 << (iota((CUBES, 256), 1) >> 5)
    bits, hots = [], []
    for h in range(HEADS):
        owner_hot = flag(owner_ref[h:h + 1, :] == iota((128, 256), 0))
        hots.append(owner_hot)
        within_bit = jnp.where(within_ref[h:h + 1, :] == iota((CUBES, 256), 0), entry_bit, 0)
        bits.append(lax.dot_general(within_bit.astype(jnp.float32).astype(jnp.bfloat16), owner_hot, NT,
                                    preferred_element_type=jnp.float32))
    bits = jnp.concatenate(bits, axis=0)
    need = bits > 0
    lower = flag(iota((UNITS, UNITS), 0) >= iota((UNITS, UNITS), 1))
    rank = jnp.dot(lower, flag(need), preferred_element_type=jnp.float32)
    bits_ref[...] = bits
    rank_ref[...] = rank
    unit = iota((UNITS, 128), 0)
    table_ref[...] = jnp.zeros_like(table_ref)
    for s in range(SLOTS):
        table_ref[s:s + 1, :] = jnp.sum(jnp.where(need & (rank == s + 1), unit, 0), axis=0, keepdims=True)
    pos_ref[...] = jnp.zeros_like(pos_ref)
    for h in range(HEADS):
        owner = owner_ref[h:h + 1, :]
        spread = jnp.dot(rank[h * 8:h * 8 + 8].astype(jnp.bfloat16), hots[h], preferred_element_type=jnp.float32)
        here = jnp.where(within_ref[h:h + 1, :] == iota((CUBES, 256), 0), spread, 0.0)
        order = jnp.sum(here, axis=0, keepdims=True).astype(jnp.int32) - 1
        ahead = (((owner >> 2) & 7) - z) & 7
        which = jnp.where(ahead == 0, 0, jnp.where(ahead >= 6, 8 - ahead, ahead + 2))
        column = (owner >> 5) * NX + (owner & 3)
        late = (ahead >= 3) & (ahead <= 5)
        pos_ref[h:h + 1, :] = jnp.where(late, -1, (which * PLANE + column) * SLOTS + order)


def head_lists(z, bits_ref, rank_ref, count_ref, slots_ref, cubes_ref):
    bits, rank = bits_ref[...], rank_ref[...]
    need = bits > 0
    ahead = (((iota((UNITS, 128), 1) >> 2) & 7) - z) & 7
    late = (ahead >= 3) & (ahead <= 5)
    mine, mine_bits = [], []
    for s in range(SLOTS):
        hit = jnp.where(need & (rank == s + 1) & late, 1.0, 0.0)
        seen = hit * bits
        mine.append([jnp.sum(hit[h * 8:h * 8 + 8], axis=0, keepdims=True) for h in range(HEADS)])
        mine_bits.append([jnp.sum(seen[h * 8:h * 8 + 8], axis=0, keepdims=True) for h in range(HEADS)])
    wide = SLOTS * 128
    upper = flag(iota((wide, wide), 0) <= iota((wide, wide), 1))
    lane = iota((1, wide), 1)
    owner = lane & 127
    ahead = (((owner >> 2) & 7) - z) & 7
    index = jnp.where(ahead == 5, 0, jnp.where(ahead == 3, 1, 2))
    place = ((owner >> 5) * NX + (owner & 3)) * len(LATE) + index
    place = jnp.broadcast_to(place.astype(jnp.float32), (8, wide))
    slot = jnp.broadcast_to((lane >> 7).astype(jnp.float32), (8, wide))
    sub = iota((8, wide), 0)
    for h in range(HEADS):
        have = jnp.concatenate([mine[s][h] for s in range(SLOTS)], axis=1)
        have_bits = jnp.concatenate([mine_bits[s][h] for s in range(SLOTS)], axis=1)
        have8 = jnp.broadcast_to(have, (8, wide))
        order = jnp.dot(have8.astype(jnp.bfloat16), upper, preferred_element_type=jnp.float32)
        want = (iota((256, wide), 0) + 1).astype(jnp.float32)
        hit = jnp.where((order[0:1, :] == want) & (have > 0), 1.0, 0.0).astype(jnp.bfloat16)
        facts = jnp.where(sub == 0, place, jnp.where(sub == 1, slot, jnp.broadcast_to(have_bits, (8, wide))))
        facts = lax.dot_general(facts.astype(jnp.bfloat16), hit, NT, preferred_element_type=jnp.float32)
        slots_ref[h:h + 1, :] = (facts[0:1, :] * SLOTS + facts[1:2, :]).astype(jnp.int32)
        cubes_ref[h:h + 1, :] = facts[2:3, :].astype(jnp.int32)
        total = jnp.sum(have, axis=1, keepdims=True)
        count_ref[h:h + 1, :] = jnp.broadcast_to(total, (1, 128)).astype(jnp.int32)


def exchange(
    q_hbm, k_hbm, v_hbm, lists_ref, recv, coarse_ref, count_ref, slots_ref, cubes_ref, part_ref, stat_ref, *scratch
):
    q_own = scratch[0]
    kk = scratch[1:9]
    vv = scratch[9:17]
    (send_buf, early, owner_rows, within_rows, tbl_ref, bits_ref, rank_ref, pos_ref, pos_sm, tbl_all, tbl_sm, q_all, pool_k, pool_v, o_res, o_half, o_got, stats, stats_all,
     load_sem, z_send, z_recv, t_send, t_recv, q_send, q_recv, u_send, u_recv,
     o_send, o_recv, m_send, m_recv, sm_sem, pos_sem, loc_sem) = scratch[17:]
    s = lax.axis_index("seq")
    x = lax.rem(s, NX)
    z = lax.rem(lax.div(s, NX), NZ)
    y = lax.div(s, NX * NZ)
    me = y * NX + x

    def peer(j):
        px = lax.rem(x + lax.rem(j, NX), NX)
        py = lax.rem(y + lax.div(j, NX), NY)
        return py * NX + px, (py * NZ + z) * NX + px

    def remote(src, dst, send, recv_, seq):
        return pltpu.make_async_remote_copy(
            src_ref=src, dst_ref=dst, send_sem=send, recv_sem=recv_,
            device_id={"seq": seq}, device_id_type=pl.DeviceIdType.MESH,
        )

    right = (y * NZ + lax.rem(z + 1, NZ)) * NX + x
    left = (y * NZ + lax.rem(z + NZ - 1, NZ)) * NX + x

    loads = []
    for i, (src, dst) in enumerate(((k_hbm, kk[0]), (v_hbm, vv[0]), (q_hbm, q_own))):
        for h in range(HEADS):
            loads.append(pltpu.make_async_copy(
                src.at[:, :, pl.ds(h * HD, HD)], dst.at[pl.ds(h * CUBES, CUBES)], load_sem.at[i * HEADS + h]))
    for c in loads:
        c.start()

    barrier = pltpu.get_barrier_semaphore()
    for seq in (right, left):
        pl.semaphore_signal(barrier, inc=1, device_id={"seq": seq}, device_id_type=pl.DeviceIdType.MESH)

    @pl.loop(1, PLANE)
    def _(j):
        pl.semaphore_signal(barrier, inc=1, device_id={"seq": peer(j)[1]}, device_id_type=pl.DeviceIdType.MESH)

    list_rows(lists_ref, owner_rows, within_rows)
    unit_slots(z, owner_rows, within_rows, tbl_ref, bits_ref, rank_ref, pos_ref)
    pl.semaphore_wait(barrier, PLANE + 1)

    @pl.loop(1, PLANE)
    def _(j):
        pp, seq = peer(j)
        remote(tbl_ref, tbl_all.at[me], t_send.at[j], t_recv.at[me], seq).start()

    def ring(first, second, base, far, seq, sem0):
        out = []
        for n in range(14):
            vals = first if n % 4 < 2 else second
            stage = n // 4
            src = vals[0 if stage == 0 else base + stage - 1]
            dst = vals[base + stage if stage < 3 else far]
            part = pl.ds((n % 2) * 24, 24)
            out.append(remote(src.at[part], dst.at[part], z_send.at[sem0 + n], z_recv.at[sem0 + n], seq))
        return out

    to_right = ring(kk, vv, 1, 7, right, 0)
    to_left = ring(vv, kk, 4, 7, left, 14)

    for c in loads[:2 * HEADS]:
        c.wait()
    for n in range(AHEAD):
        to_right[n].start()
        to_left[n].start()

    tbl_all[me] = tbl_ref[...]
    for c in loads[2 * HEADS:]:
        c.wait()

    row = lax.broadcasted_iota(jnp.int32, (CUBES, 512), 0)
    col = lax.broadcasted_iota(jnp.int32, (CUBES, 512), 1)
    mean = jnp.where(lax.div(col, TOK) == row, 1.0 / TOK, 0.0).astype(jnp.bfloat16)

    @pl.loop(0, HEADS)
    def _(h):
        q_all[me, pl.ds(h * CUBES, CUBES), :] = jnp.dot(
            mean, q_own[pl.ds(h * CUBES, CUBES)].reshape(512, HD), preferred_element_type=jnp.float32)

    @pl.loop(1, PLANE)
    def _(j):
        pp, seq = peer(j)
        remote(q_all.at[me], q_all.at[me], q_send.at[j], q_recv.at[me], seq).start()

    @pl.loop(1, PLANE)
    def _(j):
        pp, seq = peer(j)
        remote(tbl_ref, tbl_all.at[pp], t_send.at[j], t_recv.at[pp], seq).wait()

    to_smem_pos = pltpu.make_async_copy(pos_ref, pos_sm, pos_sem)
    to_smem_pos.start()
    to_smem = pltpu.make_async_copy(tbl_all, tbl_sm, sm_sem)
    to_smem.start()
    to_smem.wait()
    to_smem_pos.wait()

    def owner_z(k):
        if k <= 3:
            return lax.rem(z + NZ - k, NZ)
        if k <= 6:
            return lax.rem(z + k - 3, NZ)
        return lax.rem(z + 4, NZ)

    def unit_of(k, val, pp, sl):
        lane = (y * NZ + owner_z(k)) * NX + x
        return (vv[k] if val else kk[k])[jnp.clip(tbl_sm[pp, sl, lane], 0, UNITS - 1)]

    def landing(k, val, p):
        if k in EARLY:
            return early.at[val, pl.ds((EARLY[k] * PLANE + p) * SLOTS, SLOTS)]
        return recv.at[val, pl.ds((p * len(LATE) + LATE[k]) * SLOTS, SLOTS)]

    def own_copy(k, val):
        return pltpu.make_async_copy(send_buf.at[val, k, me], landing(k, val, me), loc_sem.at[val, LATE[k]])

    def handle(k, val):
        @pl.loop(1, PLANE)
        def _(j):
            pp, seq = peer(j)
            for sl in range(SLOTS):
                send_buf[val, k, pp, sl] = unit_of(k, val, pp, sl)
            remote(send_buf.at[val, k, pp], landing(k, val, me), u_send.at[val, k, j], u_recv.at[val, k, me], seq).start()

        for sl in range(SLOTS):
            if k in LATE:
                send_buf[val, k, me, sl] = unit_of(k, val, me, sl)
            elif k > 0:
                early[val, (EARLY[k] * PLANE + me) * SLOTS + sl] = unit_of(k, val, me, sl)
        if k in LATE:
            own_copy(k, val).start()

    def arrived(k, val):
        @pl.loop(1, PLANE)
        def _(j):
            pp, seq = peer(j)
            remote(send_buf.at[val, k, pp], landing(k, val, pp), u_send.at[val, k, j], u_recv.at[val, k, pp], seq).wait_recv()

    low_lanes = iota((1, 128), 1) < TOK

    def attend(i):
        h, c = lax.div(i, CUBES), lax.rem(i, CUBES)
        q = q_own[i]
        scores = [lax.dot_general(q, kk[0][i], NT, preferred_element_type=jnp.float32)]
        spots = [pos_sm[h, c * TOP + t] for t in range(TOP)]
        where = [jnp.clip(jnp.where(p < 0, SAFE, p), 0, len(EARLY) * PLANE * SLOTS - 1) for p in spots]
        bias = [jnp.where(p < 0, NEG, 0.0) for p in spots]
        for g in range(TOP // 4):
            keys = jnp.concatenate([early[0, where[4 * g + t]] for t in range(4)], axis=0)
            sc = lax.dot_general(q, keys, NT, preferred_element_type=jnp.float32)
            hide = jnp.concatenate(
                [jnp.where(low_lanes, bias[4 * g + t], bias[4 * g + t + 1]) for t in (0, 2)], axis=1)
            scores.append(sc + hide)
        top = functools.reduce(jnp.maximum, scores[1:])
        top = jnp.maximum(jnp.max(top, axis=1, keepdims=True), jnp.max(scores[0], axis=1, keepdims=True))
        es = [jnp.exp2((sc - top) * (SCALE * LOG2E)) for sc in scores]
        tot = jnp.sum(es[0], axis=1, keepdims=True) + jnp.sum(sum(es[2:], es[1]), axis=1, keepdims=True)
        acc = jnp.dot(es[0].astype(jnp.bfloat16), vv[0][i], preferred_element_type=jnp.float32)
        for g in range(TOP // 4):
            vals = jnp.concatenate([early[1, where[4 * g + t]] for t in range(4)], axis=0)
            acc += jnp.dot(es[g + 1].astype(jnp.bfloat16), vals, preferred_element_type=jnp.float32)
        part_ref[i] = acc
        stat_ref[i] = jnp.where(low_lanes, top, tot)

    def attend_range(lo, hi):
        @pl.loop(lo, hi)
        def _(i):
            attend(i)

    def pool(k, val):
        src, dst = (vv[k], pool_v) if val else (kk[k], pool_k)

        @pl.loop(0, HEADS)
        def _(h):
            dst[h, pl.ds(k * CUBES, CUBES), :] = jnp.dot(
                mean, src[pl.ds(h * CUBES, CUBES)].reshape(512, HD), preferred_element_type=jnp.float32)

    handle(0, 0)
    handle(0, 1)
    pool(0, 0)
    pool(0, 1)
    head_lists(z, bits_ref, rank_ref, count_ref, slots_ref, cubes_ref)
    for n in range(14):
        for way in (to_right, to_left):
            way[n].wait_recv()
            if n + AHEAD < 14:
                way[n + AHEAD].start()
        if n % 2:
            stage = n // 4
            val = (n % 4) // 2
            for k, which in ((1 + stage if stage < 3 else 7, val), (4 + stage if stage < 3 else 7, 1 - val)):
                if stage < 3:
                    handle(k, which)
                pool(k, which)
        if n == 10:
            for k in EARLY:
                arrived(k, 0)
                arrived(k, 1)
            attend_range(0, 8)
        if n == 11:
            attend_range(8, 22)
        if n == 12:
            attend_range(22, 30)

    @pl.loop(1, PLANE)
    def _(j):
        pp, seq = peer(j)
        remote(q_all.at[me], q_all.at[pp], q_send.at[j], q_recv.at[pp], seq).wait()

    lane3 = lax.broadcasted_iota(jnp.int32, (PLANE * CUBES, HD), 1)

    def coarse_head(h, stat):
        rows = pl.ds(pl.multiple_of(h * CUBES, CUBES), CUBES)
        qh = q_all[:, rows, :].reshape(PLANE * CUBES, HD)
        sc = lax.dot_general(qh, pool_k[h], NT, precision=lax.Precision.HIGHEST,
                             preferred_element_type=jnp.float32) * SCALE
        top = jnp.max(sc, axis=1, keepdims=True)
        e = jnp.exp(sc - top)
        tot = jnp.sum(e, axis=1, keepdims=True)
        o = jnp.dot(e, pool_v[h], precision=lax.Precision.HIGHEST, preferred_element_type=jnp.float32)
        o_res[:, rows, :] = o.reshape(PLANE, CUBES, HD)
        stat = jnp.where(lane3 == h, top, stat)
        return jnp.where(lane3 == h + 64, tot, stat)

    stat = lax.fori_loop(0, HEADS, coarse_head, jnp.zeros((PLANE * CUBES, HD), jnp.float32))
    stats[...] = stat.reshape(PLANE, CUBES, HD)
    o_half[...] = o_res[...].astype(jnp.bfloat16)

    @pl.loop(1, PLANE)
    def _(j):
        pp, seq = peer(j)
        remote(o_half.at[pp], o_got.at[me], o_send.at[j], o_recv.at[me], seq).start()
        remote(stats.at[pp], stats_all.at[me], m_send.at[j], m_recv.at[me], seq).start()

    handle(7, 0)
    handle(7, 1)
    attend_range(30, UNITS)
    o_got[me] = o_half[me]
    stats_all[me] = stats[me]

    @pl.loop(1, PLANE)
    def _(j):
        pp, seq = peer(j)
        remote(o_half.at[pp], o_got.at[pp], o_send.at[j], o_recv.at[pp], seq).wait()
        remote(stats.at[pp], stats_all.at[pp], m_send.at[j], m_recv.at[pp], seq).wait()

    o_res[...] = o_got[...].astype(jnp.float32)
    for h in range(HEADS):
        top = stats_all[:, :, h:h + 1]
        tot = stats_all[:, :, 64 + h:65 + h]
        w = jnp.exp(top - jnp.max(top, axis=0, keepdims=True))
        den = jnp.sum(w * tot, axis=0)
        num = jnp.sum(w * o_res[:, pl.ds(h * CUBES, CUBES), :], axis=0)
        coarse_ref[pl.ds(h * CUBES, CUBES), :] = num / den

    for c in to_right + to_left:
        c.wait_send()
    for k in range(NZ):
        for val in range(2):
            if k in LATE:
                own_copy(k, val).wait()
                arrived(k, val)

            @pl.loop(1, PLANE)
            def _(j):
                pp, seq = peer(j)
                remote(send_buf.at[val, k, pp], landing(k, val, me), u_send.at[val, k, j], u_recv.at[val, k, me], seq).wait_send()


def fine(count_ref, slot_ref, bits_ref, gate_ref, q_ref, stat_ref, coarse_ref, part_hbm, recv_hbm, out_ref,
         recv, part_ref, s_buf, top, peak, tot, acc, sem):
    c2 = SCALE * LOG2E
    pairs = GROUP // 2
    copies = [pltpu.make_async_copy(recv_hbm.at[i], recv.at[i], sem.at[i]) for i in range(2)]
    copies.append(pltpu.make_async_copy(part_hbm, part_ref, sem.at[2]))
    for c in copies:
        c.start()
    lane = lax.broadcasted_iota(jnp.int32, (1, 128), 1)

    def columns(h):
        return pl.ds(pl.multiple_of(h * HD, HD), HD)

    def blocks(h):
        return jnp.maximum(lax.div(count_ref[jnp.minimum(h, HEADS - 1), 0] + GROUP - 1, GROUP), 1)

    def step(at):
        h, g = at
        last = g + 1 >= blocks(h)
        return jnp.where(last, h + 1, h), jnp.where(last, 0, g + 1)

    def units(val, h, g):
        return jnp.concatenate(
            [recv[val, slot_ref[h, jnp.clip(count_ref[h, 0] - 1, 0, g * GROUP + t)]] for t in range(GROUP)], axis=0)

    def score(i, at):
        h, g = at
        slot = lax.rem(i, RING)
        sc = lax.dot_general(q_ref[:, columns(h)], units(0, h, g), NT, preferred_element_type=jnp.float32)
        rowbits = [
            jnp.where(lane < TOK, bits_ref[h, g * GROUP + 2 * t], bits_ref[h, g * GROUP + 2 * t + 1])
            for t in range(pairs)
        ]
        for c in range(CUBES):
            rows = pl.ds(c * TOK, TOK)
            best = top[h, rows, :]
            for t in range(pairs):
                bias = jnp.where((rowbits[t] >> c) & 1 == 1, 0.0, NEG)
                part = sc[c * TOK:(c + 1) * TOK, t * 128:(t + 1) * 128] + bias
                s_buf[slot, t, rows, :] = part
                best = jnp.maximum(best, part)
            top[h, rows, :] = best

    def begin(at):
        h, g = at

        @pl.when(g == 0)
        def _():
            peak[...] = jnp.broadcast_to(jnp.max(top[h], axis=1, keepdims=True) * c2, (CUBES * TOK, HD))
            for c in range(CUBES):
                rows = pl.ds(c * TOK, TOK)
                state = stat_ref[h * CUBES + c]
                shrink = jnp.exp2(state[:, 0:1] * c2 - peak[rows, :])
                tot[rows, :] = shrink * jnp.where(lane < TOK, 0.0, state * (1.0 / TOK))
                acc[rows, :] = shrink * part_ref[h * CUBES + c]

    def value(i, at):
        h, g = at
        slot = lax.rem(i, RING)
        blocks_of_rows = []
        for c in range(CUBES):
            rows = pl.ds(c * TOK, TOK)
            high, sums, parts = peak[rows, :], tot[rows, :], []
            for t in range(pairs):
                e = jnp.exp2(s_buf[slot, t, rows, :] * c2 - high)
                sums += e
                parts.append(e.astype(jnp.bfloat16))
            tot[rows, :] = sums
            blocks_of_rows.append(jnp.concatenate(parts, axis=1))
        acc[...] += jnp.dot(
            jnp.concatenate(blocks_of_rows, axis=0), units(1, h, g), preferred_element_type=jnp.float32)

    def finish(at):
        h, g = at

        @pl.when(g + 1 == blocks(h))
        def _():
            for c in range(CUBES):
                rows = pl.ds(c * TOK, TOK)
                total = jnp.sum(tot[rows, :], axis=1, keepdims=True)
                pooled = gate_ref[h] * coarse_ref[pl.ds(h * CUBES + c, 1), :]
                out_ref[rows, columns(h)] = (acc[rows, :] / total + pooled).astype(jnp.bfloat16)

    @pl.loop(0, UNITS)
    def _(i):
        rows = pl.ds(pl.multiple_of(lax.rem(i, CUBES) * TOK, TOK), TOK)
        top[lax.div(i, CUBES), rows, :] = jnp.where(lane < TOK, stat_ref[i], NEG)

    longest, items = blocks(0), blocks(0)
    for h in range(1, HEADS):
        longest, items = jnp.maximum(longest, blocks(h)), items + blocks(h)
    copies[0].wait()

    def only_score(i, at):
        score(i, at)
        return step(at)

    def both(i, carry):
        ahead, at = carry
        begin(at)
        value(i - longest, at)
        score(i, ahead)
        finish(at)
        return step(ahead), step(at)

    def only_value(i, at):
        begin(at)
        value(i - longest, at)
        finish(at)
        return step(at)

    zero = jnp.int32(0)
    ahead = lax.fori_loop(0, longest, only_score, (zero, zero))
    copies[1].wait()
    copies[2].wait()
    ahead, at = lax.fori_loop(longest, items, both, (ahead, (zero, zero)))
    lax.fori_loop(items, items + longest, only_value, at)


def project(att_hbm, w_hbm, out_ref, own, other, w_buf, total, send_sem, recv_sem, w_sem, own_sem):
    head = lax.axis_index("head")
    width = HEADS * HD
    weights = pltpu.make_async_copy(w_hbm.at[:, pl.ds(pl.multiple_of(head * width, width), width)], w_buf, w_sem)
    fetch = pltpu.make_async_copy(att_hbm, own, own_sem)
    fetch.start()
    weights.start()
    barrier = pltpu.get_barrier_semaphore()
    pl.semaphore_signal(barrier, inc=1, device_id={"head": 1 - head}, device_id_type=pl.DeviceIdType.MESH)
    pl.semaphore_wait(barrier, 1)
    swap = pltpu.make_async_remote_copy(
        src_ref=att_hbm, dst_ref=other, send_sem=send_sem, recv_sem=recv_sem,
        device_id={"head": 1 - head}, device_id_type=pl.DeviceIdType.MESH)
    swap.start()
    fetch.wait()
    weights.wait()
    mine = pl.ds(pl.multiple_of(head * width, width), width)
    theirs = pl.ds(pl.multiple_of((1 - head) * width, width), width)
    total[...] = jnp.dot(own[...], w_buf[mine, :], preferred_element_type=jnp.float32)
    swap.wait()
    out_ref[...] = (
        total[...] + jnp.dot(other[...], w_buf[theirs, :], preferred_element_type=jnp.float32)).astype(jnp.bfloat16)


def body(query_input, key_input, value_input, cube_lists, coarse_gate, out_weight):
    any_spec = pl.BlockSpec(memory_space=pl.ANY)
    vmem_spec = pl.BlockSpec(memory_space=pltpu.VMEM)
    smem_spec = pl.BlockSpec(memory_space=pltpu.SMEM)
    dma = pltpu.SemaphoreType.DMA
    recv, coarse, count, slots, cubes, part, stat = pl.pallas_call(
        exchange,
        out_shape=(
            jax.ShapeDtypeStruct((2, PLANE * len(LATE) * SLOTS, TOK, HD), jnp.bfloat16),
            jax.ShapeDtypeStruct((UNITS, HD), jnp.float32),
            jax.ShapeDtypeStruct((HEADS, 128), jnp.int32),
            jax.ShapeDtypeStruct((HEADS, 256), jnp.int32),
            jax.ShapeDtypeStruct((HEADS, 256), jnp.int32),
            jax.ShapeDtypeStruct((UNITS, TOK, HD), jnp.float32),
            jax.ShapeDtypeStruct((UNITS, TOK, HD), jnp.float32),
        ),
        in_specs=[any_spec] * 3 + [vmem_spec],
        out_specs=(any_spec,) + (vmem_spec,) * 6,
        scratch_shapes=[pltpu.VMEM((UNITS, TOK, HD), jnp.bfloat16)] * 17 + [
            pltpu.VMEM((2, NZ, PLANE, SLOTS, TOK, HD), jnp.bfloat16),
            pltpu.VMEM((2, len(EARLY) * PLANE * SLOTS, TOK, HD), jnp.bfloat16),
            pltpu.VMEM((8, 256), jnp.int32),
            pltpu.VMEM((8, 256), jnp.int32),
            pltpu.VMEM((8, 128), jnp.int32),
            pltpu.VMEM((UNITS, 128), jnp.float32),
            pltpu.VMEM((UNITS, 128), jnp.float32),
            pltpu.VMEM((8, 256), jnp.int32),
            pltpu.SMEM((8, 256), jnp.int32),
            pltpu.VMEM((PLANE, 8, 128), jnp.int32),
            pltpu.SMEM((PLANE, 8, 128), jnp.int32),
            pltpu.VMEM((PLANE, UNITS, HD), jnp.float32),
            pltpu.VMEM((HEADS, NZ * CUBES, HD), jnp.float32),
            pltpu.VMEM((HEADS, NZ * CUBES, HD), jnp.float32),
            pltpu.VMEM((PLANE, UNITS, HD), jnp.float32),
            pltpu.VMEM((PLANE, UNITS, HD), jnp.bfloat16),
            pltpu.VMEM((PLANE, UNITS, HD), jnp.bfloat16),
            pltpu.VMEM((PLANE, CUBES, HD), jnp.float32),
            pltpu.VMEM((PLANE, CUBES, HD), jnp.float32),
            dma((18,)), dma((28,)), dma((28,)), dma((PLANE,)), dma((PLANE,)), dma((PLANE,)), dma((PLANE,)),
            dma((2, NZ, PLANE)), dma((2, NZ, PLANE)), dma((PLANE,)), dma((PLANE,)), dma((PLANE,)), dma((PLANE,)), dma, dma, dma((2, len(LATE))),
        ],
        compiler_params=pltpu.CompilerParams(
            collective_id=0, has_side_effects=True, vmem_limit_bytes=44 * 1024 * 1024),
        name="exchange",
    )(*[t.reshape(CUBES, TOK, HEADS * HD) for t in (query_input, key_input, value_input)],
      jnp.transpose(cube_lists, (1, 0, 2)))
    attended = pl.pallas_call(
        fine,
        out_shape=jax.ShapeDtypeStruct((CUBES * TOK, HEADS * HD), jnp.bfloat16),
        in_specs=[smem_spec] * 4 + [vmem_spec] * 3 + [any_spec] * 2,
        out_specs=vmem_spec,
        scratch_shapes=[
            pltpu.VMEM((2, PLANE * len(LATE) * SLOTS, TOK, HD), jnp.bfloat16),
            pltpu.VMEM((UNITS, TOK, HD), jnp.float32),
            pltpu.VMEM((RING, GROUP // 2, CUBES * TOK, HD), jnp.float32),
        ] + [pltpu.VMEM((HEADS, CUBES * TOK, HD), jnp.float32)] + [pltpu.VMEM((CUBES * TOK, HD), jnp.float32)] * 3
        + [dma((3,))],
        compiler_params=pltpu.CompilerParams(vmem_limit_bytes=40 * 1024 * 1024),
        name="fine",
    )(count, slots, cubes, coarse_gate, query_input, stat, coarse, part, recv)
    shape = (CUBES * TOK, HEADS * HD)
    return pl.pallas_call(
        project,
        out_shape=jax.ShapeDtypeStruct(shape, jnp.bfloat16),
        in_specs=[pl.BlockSpec(memory_space=pltpu.HBM)] * 2,
        out_specs=vmem_spec,
        scratch_shapes=[
            pltpu.VMEM(shape, jnp.bfloat16),
            pltpu.VMEM(shape, jnp.bfloat16),
            pltpu.VMEM((2 * HEADS * HD, HEADS * HD), jnp.bfloat16),
            pltpu.VMEM(shape, jnp.float32),
            dma, dma, dma, dma,
        ],
        compiler_params=pltpu.CompilerParams(
            collective_id=1, has_side_effects=True, vmem_limit_bytes=48 * 1024 * 1024),
        name="project",
    )(attended, out_weight)


def solution(mesh):
    placed = (
        P("seq", "head"),
        P("seq", "head"),
        P("seq", "head"),
        P("seq", "head", None),
        P("head"),
        P(),
    )
    return jax.shard_map(
        body, mesh=mesh, in_specs=placed, out_specs=P("seq", "head"), check_vma=False
    )
```

```python
import functools

import jax
import jax.numpy as jnp
from jax import lax
from jax.experimental import pallas as pl
from jax.experimental.pallas import tpu as pltpu
from jax.sharding import PartitionSpec as P

NX, NY, NZ = 4, 4, 8
PLANE = NX * NY
SLOTS = 3
CUBES = 8
HEADS = 6
TOK = 64
HD = 128
TOP = 32
UNITS = CUBES * HEADS
MAXU = 144
GROUP = 4
RING = MAXU // GROUP
NEG = -1e30
AHEAD = 4
EARLY = {0: 0, 1: 1, 2: 2, 4: 3, 5: 4}
LATE = {3: 0, 6: 1, 7: 2}
SAFE = PLANE * SLOTS
SCALE = HD ** -0.5
LOG2E = 1.4426950408889634
NT = (((1,), (1,)), ((), ()))


def iota(shape, dim):
    return lax.broadcasted_iota(jnp.int32, shape, dim)


def flag(mask):
    return jnp.where(mask, 1.0, 0.0).astype(jnp.bfloat16)


def list_rows(lists_ref, owner_ref, within_ref):
    spread = flag((iota((TOP, 256), 1) & (TOP - 1)) == iota((TOP, 256), 0))
    mine = (iota((CUBES, 256), 1) >> 5) == iota((CUBES, 256), 0)
    for h in range(HEADS):
        cubes = lists_ref[h]
        for part, ref in ((cubes >> 3, owner_ref), (cubes & 7, within_ref)):
            wide = jnp.dot(part.astype(jnp.float32).astype(jnp.bfloat16), spread, preferred_element_type=jnp.float32)
            ref[h:h + 1, :] = jnp.sum(jnp.where(mine, wide, 0.0), axis=0, keepdims=True).astype(jnp.int32)


def unit_slots(z, owner_ref, within_ref, table_ref, bits_ref, rank_ref, pos_ref):
    entry_bit = 1 << (iota((CUBES, 256), 1) >> 5)
    bits, hots = [], []
    for h in range(HEADS):
        owner_hot = flag(owner_ref[h:h + 1, :] == iota((128, 256), 0))
        hots.append(owner_hot)
        within_bit = jnp.where(within_ref[h:h + 1, :] == iota((CUBES, 256), 0), entry_bit, 0)
        bits.append(lax.dot_general(within_bit.astype(jnp.float32).astype(jnp.bfloat16), owner_hot, NT,
                                    preferred_element_type=jnp.float32))
    bits = jnp.concatenate(bits, axis=0)
    need = bits > 0
    lower = flag(iota((UNITS, UNITS), 0) >= iota((UNITS, UNITS), 1))
    rank = jnp.dot(lower, flag(need), preferred_element_type=jnp.float32)
    bits_ref[...] = bits
    rank_ref[...] = rank
    unit = iota((UNITS, 128), 0)
    table_ref[...] = jnp.zeros_like(table_ref)
    for s in range(SLOTS):
        table_ref[s:s + 1, :] = jnp.sum(jnp.where(need & (rank == s + 1), unit, 0), axis=0, keepdims=True)
    pos_ref[...] = jnp.zeros_like(pos_ref)
    for h in range(HEADS):
        owner = owner_ref[h:h + 1, :]
        spread = jnp.dot(rank[h * 8:h * 8 + 8].astype(jnp.bfloat16), hots[h], preferred_element_type=jnp.float32)
        here = jnp.where(within_ref[h:h + 1, :] == iota((CUBES, 256), 0), spread, 0.0)
        order = jnp.sum(here, axis=0, keepdims=True).astype(jnp.int32) - 1
        ahead = (((owner >> 2) & 7) - z) & 7
        which = jnp.where(ahead == 0, 0, jnp.where(ahead >= 6, 8 - ahead, ahead + 2))
        column = (owner >> 5) * NX + (owner & 3)
        late = (ahead >= 3) & (ahead <= 5)
        pos_ref[h:h + 1, :] = jnp.where(late, -1, (which * PLANE + column) * SLOTS + order)


def head_lists(z, bits_ref, rank_ref, count_ref, slots_ref, cubes_ref):
    bits, rank = bits_ref[...], rank_ref[...]
    need = bits > 0
    ahead = (((iota((UNITS, 128), 1) >> 2) & 7) - z) & 7
    late = (ahead >= 3) & (ahead <= 5)
    mine, mine_bits = [], []
    for s in range(SLOTS):
        hit = jnp.where(need & (rank == s + 1) & late, 1.0, 0.0)
        seen = hit * bits
        mine.append([jnp.sum(hit[h * 8:h * 8 + 8], axis=0, keepdims=True) for h in range(HEADS)])
        mine_bits.append([jnp.sum(seen[h * 8:h * 8 + 8], axis=0, keepdims=True) for h in range(HEADS)])
    wide = SLOTS * 128
    upper = flag(iota((wide, wide), 0) <= iota((wide, wide), 1))
    lane = iota((1, wide), 1)
    owner = lane & 127
    ahead = (((owner >> 2) & 7) - z) & 7
    index = jnp.where(ahead == 5, 0, jnp.where(ahead == 3, 1, 2))
    place = ((owner >> 5) * NX + (owner & 3)) * len(LATE) + index
    place = jnp.broadcast_to(place.astype(jnp.float32), (8, wide))
    slot = jnp.broadcast_to((lane >> 7).astype(jnp.float32), (8, wide))
    sub = iota((8, wide), 0)
    for h in range(HEADS):
        have = jnp.concatenate([mine[s][h] for s in range(SLOTS)], axis=1)
        have_bits = jnp.concatenate([mine_bits[s][h] for s in range(SLOTS)], axis=1)
        have8 = jnp.broadcast_to(have, (8, wide))
        order = jnp.dot(have8.astype(jnp.bfloat16), upper, preferred_element_type=jnp.float32)
        want = (iota((256, wide), 0) + 1).astype(jnp.float32)
        hit = jnp.where((order[0:1, :] == want) & (have > 0), 1.0, 0.0).astype(jnp.bfloat16)
        facts = jnp.where(sub == 0, place, jnp.where(sub == 1, slot, jnp.broadcast_to(have_bits, (8, wide))))
        facts = lax.dot_general(facts.astype(jnp.bfloat16), hit, NT, preferred_element_type=jnp.float32)
        slots_ref[h:h + 1, :] = (facts[0:1, :] * SLOTS + facts[1:2, :]).astype(jnp.int32)
        cubes_ref[h:h + 1, :] = facts[2:3, :].astype(jnp.int32)
        total = jnp.sum(have, axis=1, keepdims=True)
        count_ref[h:h + 1, :] = jnp.broadcast_to(total, (1, 128)).astype(jnp.int32)


def exchange(
    q_hbm, k_hbm, v_hbm, lists_ref, recv, coarse_ref, count_ref, slots_ref, cubes_ref, part_ref, stat_ref, *scratch
):
    q_own = scratch[0]
    kk = scratch[1:9]
    vv = scratch[9:17]
    (send_buf, early, owner_rows, within_rows, tbl_ref, bits_ref, rank_ref, pos_ref, pos_sm, tbl_all, tbl_sm, q_all, pool_k, pool_v, o_res, o_half, o_got, stats, stats_all,
     load_sem, z_send, z_recv, t_send, t_recv, q_send, q_recv, u_send, u_recv,
     o_send, o_recv, m_send, m_recv, sm_sem, pos_sem, loc_sem) = scratch[17:]
    s = lax.axis_index("seq")
    x = lax.rem(s, NX)
    z = lax.rem(lax.div(s, NX), NZ)
    y = lax.div(s, NX * NZ)
    me = y * NX + x

    def peer(j):
        px = lax.rem(x + lax.rem(j, NX), NX)
        py = lax.rem(y + lax.div(j, NX), NY)
        return py * NX + px, (py * NZ + z) * NX + px

    def remote(src, dst, send, recv_, seq):
        return pltpu.make_async_remote_copy(
            src_ref=src, dst_ref=dst, send_sem=send, recv_sem=recv_,
            device_id={"seq": seq}, device_id_type=pl.DeviceIdType.MESH,
        )

    right = (y * NZ + lax.rem(z + 1, NZ)) * NX + x
    left = (y * NZ + lax.rem(z + NZ - 1, NZ)) * NX + x

    loads = []
    for i, (src, dst) in enumerate(((k_hbm, kk[0]), (v_hbm, vv[0]), (q_hbm, q_own))):
        for h in range(HEADS):
            loads.append(pltpu.make_async_copy(
                src.at[:, :, pl.ds(h * HD, HD)], dst.at[pl.ds(h * CUBES, CUBES)], load_sem.at[i * HEADS + h]))
    for c in loads:
        c.start()

    barrier = pltpu.get_barrier_semaphore()
    for seq in (right, left):
        pl.semaphore_signal(barrier, inc=1, device_id={"seq": seq}, device_id_type=pl.DeviceIdType.MESH)

    @pl.loop(1, PLANE)
    def _(j):
        pl.semaphore_signal(barrier, inc=1, device_id={"seq": peer(j)[1]}, device_id_type=pl.DeviceIdType.MESH)

    list_rows(lists_ref, owner_rows, within_rows)
    unit_slots(z, owner_rows, within_rows, tbl_ref, bits_ref, rank_ref, pos_ref)
    pl.semaphore_wait(barrier, PLANE + 1)

    @pl.loop(1, PLANE)
    def _(j):
        pp, seq = peer(j)
        remote(tbl_ref, tbl_all.at[me], t_send.at[j], t_recv.at[me], seq).start()

    def ring(first, second, base, far, seq, sem0):
        out = []
        for n in range(14):
            vals = first if n % 4 < 2 else second
            stage = n // 4
            src = vals[0 if stage == 0 else base + stage - 1]
            dst = vals[base + stage if stage < 3 else far]
            part = pl.ds((n % 2) * 24, 24)
            out.append(remote(src.at[part], dst.at[part], z_send.at[sem0 + n], z_recv.at[sem0 + n], seq))
        return out

    to_right = ring(kk, vv, 1, 7, right, 0)
    to_left = ring(vv, kk, 4, 7, left, 14)

    for c in loads[:2 * HEADS]:
        c.wait()
    for n in range(AHEAD):
        to_right[n].start()
        to_left[n].start()

    tbl_all[me] = tbl_ref[...]
    for c in loads[2 * HEADS:]:
        c.wait()

    row = lax.broadcasted_iota(jnp.int32, (CUBES, 512), 0)
    col = lax.broadcasted_iota(jnp.int32, (CUBES, 512), 1)
    mean = jnp.where(lax.div(col, TOK) == row, 1.0 / TOK, 0.0).astype(jnp.bfloat16)

    @pl.loop(0, HEADS)
    def _(h):
        q_all[me, pl.ds(h * CUBES, CUBES), :] = jnp.dot(
            mean, q_own[pl.ds(h * CUBES, CUBES)].reshape(512, HD), preferred_element_type=jnp.float32)

    @pl.loop(1, PLANE)
    def _(j):
        pp, seq = peer(j)
        remote(q_all.at[me], q_all.at[me], q_send.at[j], q_recv.at[me], seq).start()

    @pl.loop(1, PLANE)
    def _(j):
        pp, seq = peer(j)
        remote(tbl_ref, tbl_all.at[pp], t_send.at[j], t_recv.at[pp], seq).wait()

    to_smem_pos = pltpu.make_async_copy(pos_ref, pos_sm, pos_sem)
    to_smem_pos.start()
    to_smem = pltpu.make_async_copy(tbl_all, tbl_sm, sm_sem)
    to_smem.start()
    to_smem.wait()
    to_smem_pos.wait()

    def owner_z(k):
        if k <= 3:
            return lax.rem(z + NZ - k, NZ)
        if k <= 6:
            return lax.rem(z + k - 3, NZ)
        return lax.rem(z + 4, NZ)

    def unit_of(k, val, pp, sl):
        lane = (y * NZ + owner_z(k)) * NX + x
        return (vv[k] if val else kk[k])[jnp.clip(tbl_sm[pp, sl, lane], 0, UNITS - 1)]

    def landing(k, val, p):
        if k in EARLY:
            return early.at[val, pl.ds((EARLY[k] * PLANE + p) * SLOTS, SLOTS)]
        return recv.at[val, pl.ds((p * len(LATE) + LATE[k]) * SLOTS, SLOTS)]

    def own_copy(k, val):
        return pltpu.make_async_copy(send_buf.at[val, k, me], landing(k, val, me), loc_sem.at[val, LATE[k]])

    def handle(k, val):
        @pl.loop(1, PLANE)
        def _(j):
            pp, seq = peer(j)
            for sl in range(SLOTS):
                send_buf[val, k, pp, sl] = unit_of(k, val, pp, sl)
            remote(send_buf.at[val, k, pp], landing(k, val, me), u_send.at[val, k, j], u_recv.at[val, k, me], seq).start()

        for sl in range(SLOTS):
            if k in LATE:
                send_buf[val, k, me, sl] = unit_of(k, val, me, sl)
            elif k > 0:
                early[val, (EARLY[k] * PLANE + me) * SLOTS + sl] = unit_of(k, val, me, sl)
        if k in LATE:
            own_copy(k, val).start()

    def arrived(k, val):
        @pl.loop(1, PLANE)
        def _(j):
            pp, seq = peer(j)
            remote(send_buf.at[val, k, pp], landing(k, val, pp), u_send.at[val, k, j], u_recv.at[val, k, pp], seq).wait_recv()

    low_lanes = iota((1, 128), 1) < TOK

    def attend(i):
        h, c = lax.div(i, CUBES), lax.rem(i, CUBES)
        q = q_own[i]
        scores = [lax.dot_general(q, kk[0][i], NT, preferred_element_type=jnp.float32)]
        spots = [pos_sm[h, c * TOP + t] for t in range(TOP)]
        where = [jnp.clip(jnp.where(p < 0, SAFE, p), 0, len(EARLY) * PLANE * SLOTS - 1) for p in spots]
        bias = [jnp.where(p < 0, NEG, 0.0) for p in spots]
        for g in range(TOP // 4):
            keys = jnp.concatenate([early[0, where[4 * g + t]] for t in range(4)], axis=0)
            sc = lax.dot_general(q, keys, NT, preferred_element_type=jnp.float32)
            hide = jnp.concatenate(
                [jnp.where(low_lanes, bias[4 * g + t], bias[4 * g + t + 1]) for t in (0, 2)], axis=1)
            scores.append(sc + hide)
        top = functools.reduce(jnp.maximum, scores[1:])
        top = jnp.maximum(jnp.max(top, axis=1, keepdims=True), jnp.max(scores[0], axis=1, keepdims=True))
        es = [jnp.exp2((sc - top) * (SCALE * LOG2E)) for sc in scores]
        tot = jnp.sum(es[0], axis=1, keepdims=True) + jnp.sum(sum(es[2:], es[1]), axis=1, keepdims=True)
        acc = jnp.dot(es[0].astype(jnp.bfloat16), vv[0][i], preferred_element_type=jnp.float32)
        for g in range(TOP // 4):
            vals = jnp.concatenate([early[1, where[4 * g + t]] for t in range(4)], axis=0)
            acc += jnp.dot(es[g + 1].astype(jnp.bfloat16), vals, preferred_element_type=jnp.float32)
        part_ref[i] = acc
        stat_ref[i] = jnp.where(low_lanes, top, tot)

    def attend_range(lo, hi):
        @pl.loop(lo, hi)
        def _(i):
            attend(i)

    def pool(k, val):
        src, dst = (vv[k], pool_v) if val else (kk[k], pool_k)

        @pl.loop(0, HEADS)
        def _(h):
            dst[h, pl.ds(k * CUBES, CUBES), :] = jnp.dot(
                mean, src[pl.ds(h * CUBES, CUBES)].reshape(512, HD), preferred_element_type=jnp.float32)

    handle(0, 0)
    handle(0, 1)
    pool(0, 0)
    pool(0, 1)
    head_lists(z, bits_ref, rank_ref, count_ref, slots_ref, cubes_ref)
    for n in range(14):
        for way in (to_right, to_left):
            way[n].wait_recv()
            if n + AHEAD < 14:
                way[n + AHEAD].start()
        if n % 2:
            stage = n // 4
            val = (n % 4) // 2
            for k, which in ((1 + stage if stage < 3 else 7, val), (4 + stage if stage < 3 else 7, 1 - val)):
                if stage < 3:
                    handle(k, which)
                pool(k, which)
        if n == 10:
            for k in EARLY:
                arrived(k, 0)
                arrived(k, 1)
            attend_range(0, 8)
        if n == 11:
            attend_range(8, 22)
        if n == 12:
            attend_range(22, 30)

    @pl.loop(1, PLANE)
    def _(j):
        pp, seq = peer(j)
        remote(q_all.at[me], q_all.at[pp], q_send.at[j], q_recv.at[pp], seq).wait()

    lane3 = lax.broadcasted_iota(jnp.int32, (PLANE * CUBES, HD), 1)

    def coarse_head(h, stat):
        rows = pl.ds(pl.multiple_of(h * CUBES, CUBES), CUBES)
        qh = q_all[:, rows, :].reshape(PLANE * CUBES, HD)
        sc = lax.dot_general(qh, pool_k[h], NT, precision=lax.Precision.HIGHEST,
                             preferred_element_type=jnp.float32) * SCALE
        top = jnp.max(sc, axis=1, keepdims=True)
        e = jnp.exp(sc - top)
        tot = jnp.sum(e, axis=1, keepdims=True)
        o = jnp.dot(e, pool_v[h], precision=lax.Precision.HIGHEST, preferred_element_type=jnp.float32)
        o_res[:, rows, :] = o.reshape(PLANE, CUBES, HD)
        stat = jnp.where(lane3 == h, top, stat)
        return jnp.where(lane3 == h + 64, tot, stat)

    stat = lax.fori_loop(0, HEADS, coarse_head, jnp.zeros((PLANE * CUBES, HD), jnp.float32))
    stats[...] = stat.reshape(PLANE, CUBES, HD)
    o_half[...] = o_res[...].astype(jnp.bfloat16)

    @pl.loop(1, PLANE)
    def _(j):
        pp, seq = peer(j)
        remote(o_half.at[pp], o_got.at[me], o_send.at[j], o_recv.at[me], seq).start()
        remote(stats.at[pp], stats_all.at[me], m_send.at[j], m_recv.at[me], seq).start()

    handle(7, 0)
    handle(7, 1)
    attend_range(30, UNITS)
    o_got[me] = o_half[me]
    stats_all[me] = stats[me]

    @pl.loop(1, PLANE)
    def _(j):
        pp, seq = peer(j)
        remote(o_half.at[pp], o_got.at[pp], o_send.at[j], o_recv.at[pp], seq).wait()
        remote(stats.at[pp], stats_all.at[pp], m_send.at[j], m_recv.at[pp], seq).wait()

    o_res[...] = o_got[...].astype(jnp.float32)
    for h in range(HEADS):
        top = stats_all[:, :, h:h + 1]
        tot = stats_all[:, :, 64 + h:65 + h]
        w = jnp.exp(top - jnp.max(top, axis=0, keepdims=True))
        den = jnp.sum(w * tot, axis=0)
        num = jnp.sum(w * o_res[:, pl.ds(h * CUBES, CUBES), :], axis=0)
        coarse_ref[pl.ds(h * CUBES, CUBES), :] = num / den

    for c in to_right + to_left:
        c.wait_send()
    for k in range(NZ):
        for val in range(2):
            if k in LATE:
                own_copy(k, val).wait()
                arrived(k, val)

            @pl.loop(1, PLANE)
            def _(j):
                pp, seq = peer(j)
                remote(send_buf.at[val, k, pp], landing(k, val, me), u_send.at[val, k, j], u_recv.at[val, k, me], seq).wait_send()


def fine(count_ref, slot_ref, bits_ref, gate_ref, q_ref, stat_ref, coarse_ref, part_hbm, recv_hbm, out_ref,
         recv, part_ref, s_buf, top, peak, tot, acc, sem):
    c2 = SCALE * LOG2E
    pairs = GROUP // 2
    copies = [pltpu.make_async_copy(recv_hbm.at[i], recv.at[i], sem.at[i]) for i in range(2)]
    copies.append(pltpu.make_async_copy(part_hbm, part_ref, sem.at[2]))
    for c in copies:
        c.start()
    lane = lax.broadcasted_iota(jnp.int32, (1, 128), 1)

    def columns(h):
        return pl.ds(pl.multiple_of(h * HD, HD), HD)

    def blocks(h):
        return jnp.maximum(lax.div(count_ref[jnp.minimum(h, HEADS - 1), 0] + GROUP - 1, GROUP), 1)

    def step(at):
        h, g = at
        last = g + 1 >= blocks(h)
        return jnp.where(last, h + 1, h), jnp.where(last, 0, g + 1)

    def units(val, h, g):
        return jnp.concatenate(
            [recv[val, slot_ref[h, jnp.clip(count_ref[h, 0] - 1, 0, g * GROUP + t)]] for t in range(GROUP)], axis=0)

    def score(i, at):
        h, g = at
        slot = lax.rem(i, RING)
        sc = lax.dot_general(q_ref[:, columns(h)], units(0, h, g), NT, preferred_element_type=jnp.float32)
        rowbits = [
            jnp.where(lane < TOK, bits_ref[h, g * GROUP + 2 * t], bits_ref[h, g * GROUP + 2 * t + 1])
            for t in range(pairs)
        ]
        for c in range(CUBES):
            rows = pl.ds(c * TOK, TOK)
            best = top[h, rows, :]
            for t in range(pairs):
                bias = jnp.where((rowbits[t] >> c) & 1 == 1, 0.0, NEG)
                part = sc[c * TOK:(c + 1) * TOK, t * 128:(t + 1) * 128] + bias
                s_buf[slot, t, rows, :] = part
                best = jnp.maximum(best, part)
            top[h, rows, :] = best

    def begin(at):
        h, g = at

        @pl.when(g == 0)
        def _():
            peak[...] = jnp.broadcast_to(jnp.max(top[h], axis=1, keepdims=True) * c2, (CUBES * TOK, HD))
            for c in range(CUBES):
                rows = pl.ds(c * TOK, TOK)
                state = stat_ref[h * CUBES + c]
                shrink = jnp.exp2(state[:, 0:1] * c2 - peak[rows, :])
                tot[rows, :] = shrink * jnp.where(lane < TOK, 0.0, state * (1.0 / TOK))
                acc[rows, :] = shrink * part_ref[h * CUBES + c]

    def value(i, at):
        h, g = at
        slot = lax.rem(i, RING)
        blocks_of_rows = []
        for c in range(CUBES):
            rows = pl.ds(c * TOK, TOK)
            high, sums, parts = peak[rows, :], tot[rows, :], []
            for t in range(pairs):
                e = jnp.exp2(s_buf[slot, t, rows, :] * c2 - high)
                sums += e
                parts.append(e.astype(jnp.bfloat16))
            tot[rows, :] = sums
            blocks_of_rows.append(jnp.concatenate(parts, axis=1))
        acc[...] += jnp.dot(
            jnp.concatenate(blocks_of_rows, axis=0), units(1, h, g), preferred_element_type=jnp.float32)

    def finish(at):
        h, g = at

        @pl.when(g + 1 == blocks(h))
        def _():
            for c in range(CUBES):
                rows = pl.ds(c * TOK, TOK)
                total = jnp.sum(tot[rows, :], axis=1, keepdims=True)
                pooled = gate_ref[h] * coarse_ref[pl.ds(h * CUBES + c, 1), :]
                out_ref[rows, columns(h)] = (acc[rows, :] / total + pooled).astype(jnp.bfloat16)

    @pl.loop(0, UNITS)
    def _(i):
        rows = pl.ds(pl.multiple_of(lax.rem(i, CUBES) * TOK, TOK), TOK)
        top[lax.div(i, CUBES), rows, :] = jnp.where(lane < TOK, stat_ref[i], NEG)

    longest, items = blocks(0), blocks(0)
    for h in range(1, HEADS):
        longest, items = jnp.maximum(longest, blocks(h)), items + blocks(h)
    copies[0].wait()

    def only_score(i, at):
        score(i, at)
        return step(at)

    def both(i, carry):
        ahead, at = carry
        begin(at)
        value(i - longest, at)
        score(i, ahead)
        finish(at)
        return step(ahead), step(at)

    def only_value(i, at):
        begin(at)
        value(i - longest, at)
        finish(at)
        return step(at)

    zero = jnp.int32(0)
    ahead = lax.fori_loop(0, longest, only_score, (zero, zero))
    copies[1].wait()
    copies[2].wait()
    ahead, at = lax.fori_loop(longest, items, both, (ahead, (zero, zero)))
    lax.fori_loop(items, items + longest, only_value, at)


def project(att_hbm, w_hbm, out_ref, own, other, w_buf, total, send_sem, recv_sem, w_sem, own_sem):
    head = lax.axis_index("head")
    width = HEADS * HD
    weights = pltpu.make_async_copy(w_hbm.at[:, pl.ds(pl.multiple_of(head * width, width), width)], w_buf, w_sem)
    fetch = pltpu.make_async_copy(att_hbm, own, own_sem)
    fetch.start()
    weights.start()
    barrier = pltpu.get_barrier_semaphore()
    pl.semaphore_signal(barrier, inc=1, device_id={"head": 1 - head}, device_id_type=pl.DeviceIdType.MESH)
    pl.semaphore_wait(barrier, 1)
    swap = pltpu.make_async_remote_copy(
        src_ref=att_hbm, dst_ref=other, send_sem=send_sem, recv_sem=recv_sem,
        device_id={"head": 1 - head}, device_id_type=pl.DeviceIdType.MESH)
    swap.start()
    fetch.wait()
    weights.wait()
    mine = pl.ds(pl.multiple_of(head * width, width), width)
    theirs = pl.ds(pl.multiple_of((1 - head) * width, width), width)
    total[...] = jnp.dot(own[...], w_buf[mine, :], preferred_element_type=jnp.float32)
    swap.wait()
    out_ref[...] = (
        total[...] + jnp.dot(other[...], w_buf[theirs, :], preferred_element_type=jnp.float32)).astype(jnp.bfloat16)


def body(query_input, key_input, value_input, cube_lists, coarse_gate, out_weight):
    any_spec = pl.BlockSpec(memory_space=pl.ANY)
    vmem_spec = pl.BlockSpec(memory_space=pltpu.VMEM)
    smem_spec = pl.BlockSpec(memory_space=pltpu.SMEM)
    dma = pltpu.SemaphoreType.DMA
    recv, coarse, count, slots, cubes, part, stat = pl.pallas_call(
        exchange,
        out_shape=(
            jax.ShapeDtypeStruct((2, PLANE * len(LATE) * SLOTS, TOK, HD), jnp.bfloat16),
            jax.ShapeDtypeStruct((UNITS, HD), jnp.float32),
            jax.ShapeDtypeStruct((HEADS, 128), jnp.int32),
            jax.ShapeDtypeStruct((HEADS, 256), jnp.int32),
            jax.ShapeDtypeStruct((HEADS, 256), jnp.int32),
            jax.ShapeDtypeStruct((UNITS, TOK, HD), jnp.float32),
            jax.ShapeDtypeStruct((UNITS, TOK, HD), jnp.float32),
        ),
        in_specs=[any_spec] * 3 + [vmem_spec],
        out_specs=(any_spec,) + (vmem_spec,) * 6,
        scratch_shapes=[pltpu.VMEM((UNITS, TOK, HD), jnp.bfloat16)] * 17 + [
            pltpu.VMEM((2, NZ, PLANE, SLOTS, TOK, HD), jnp.bfloat16),
            pltpu.VMEM((2, len(EARLY) * PLANE * SLOTS, TOK, HD), jnp.bfloat16),
            pltpu.VMEM((8, 256), jnp.int32),
            pltpu.VMEM((8, 256), jnp.int32),
            pltpu.VMEM((8, 128), jnp.int32),
            pltpu.VMEM((UNITS, 128), jnp.float32),
            pltpu.VMEM((UNITS, 128), jnp.float32),
            pltpu.VMEM((8, 256), jnp.int32),
            pltpu.SMEM((8, 256), jnp.int32),
            pltpu.VMEM((PLANE, 8, 128), jnp.int32),
            pltpu.SMEM((PLANE, 8, 128), jnp.int32),
            pltpu.VMEM((PLANE, UNITS, HD), jnp.float32),
            pltpu.VMEM((HEADS, NZ * CUBES, HD), jnp.float32),
            pltpu.VMEM((HEADS, NZ * CUBES, HD), jnp.float32),
            pltpu.VMEM((PLANE, UNITS, HD), jnp.float32),
            pltpu.VMEM((PLANE, UNITS, HD), jnp.bfloat16),
            pltpu.VMEM((PLANE, UNITS, HD), jnp.bfloat16),
            pltpu.VMEM((PLANE, CUBES, HD), jnp.float32),
            pltpu.VMEM((PLANE, CUBES, HD), jnp.float32),
            dma((18,)), dma((28,)), dma((28,)), dma((PLANE,)), dma((PLANE,)), dma((PLANE,)), dma((PLANE,)),
            dma((2, NZ, PLANE)), dma((2, NZ, PLANE)), dma((PLANE,)), dma((PLANE,)), dma((PLANE,)), dma((PLANE,)), dma, dma, dma((2, len(LATE))),
        ],
        compiler_params=pltpu.CompilerParams(
            collective_id=0, has_side_effects=True, vmem_limit_bytes=44 * 1024 * 1024),
        name="exchange",
    )(*[t.reshape(CUBES, TOK, HEADS * HD) for t in (query_input, key_input, value_input)],
      jnp.transpose(cube_lists, (1, 0, 2)))
    attended = pl.pallas_call(
        fine,
        out_shape=jax.ShapeDtypeStruct((CUBES * TOK, HEADS * HD), jnp.bfloat16),
        in_specs=[smem_spec] * 4 + [vmem_spec] * 3 + [any_spec] * 2,
        out_specs=vmem_spec,
        scratch_shapes=[
            pltpu.VMEM((2, PLANE * len(LATE) * SLOTS, TOK, HD), jnp.bfloat16),
            pltpu.VMEM((UNITS, TOK, HD), jnp.float32),
            pltpu.VMEM((RING, GROUP // 2, CUBES * TOK, HD), jnp.float32),
        ] + [pltpu.VMEM((HEADS, CUBES * TOK, HD), jnp.float32)] + [pltpu.VMEM((CUBES * TOK, HD), jnp.float32)] * 3
        + [dma((3,))],
        compiler_params=pltpu.CompilerParams(vmem_limit_bytes=40 * 1024 * 1024),
        name="fine",
    )(count, slots, cubes, coarse_gate, query_input, stat, coarse, part, recv)
    shape = (CUBES * TOK, HEADS * HD)
    return pl.pallas_call(
        project,
        out_shape=jax.ShapeDtypeStruct(shape, jnp.bfloat16),
        in_specs=[pl.BlockSpec(memory_space=pltpu.HBM)] * 2,
        out_specs=vmem_spec,
        scratch_shapes=[
            pltpu.VMEM(shape, jnp.bfloat16),
            pltpu.VMEM(shape, jnp.bfloat16),
            pltpu.VMEM((2 * HEADS * HD, HEADS * HD), jnp.bfloat16),
            pltpu.VMEM(shape, jnp.float32),
            dma, dma, dma, dma,
        ],
        compiler_params=pltpu.CompilerParams(
            collective_id=1, has_side_effects=True, vmem_limit_bytes=48 * 1024 * 1024),
        name="project",
    )(attended, out_weight)


def solution(mesh):
    placed = (
        P("seq", "head"),
        P("seq", "head"),
        P("seq", "head"),
        P("seq", "head", None),
        P("head"),
        P(),
    )
    return jax.shard_map(
        body, mesh=mesh, in_specs=placed, out_specs=P("seq", "head"), check_vma=False
    )
```
